32 devices in a mesh: seq: 8 (over z, core), tp: 4 (over y, x).
Axes of the slice: x: 2, y: 2, z: 4, core: 2. Of those that a mesh axis runs over, the one named last changes fastest.
Arguments:
- tokens: bfloat16 [4, 1024, 4096], P(None, 'seq', 'tp'), may hold values from -6 to 6
- new_tokens: bfloat16 [4, 4096], P(None, 'tp'), may hold values from -6 to 6
- w_qkv: bfloat16 [3, 4096, 4096], P(None, None, 'tp')
- w_out: bfloat16 [4096, 4096], P('tp')
- q_gain: float32 [4096], P('tp'), may hold values from 0.5 to 6
- k_gain: float32 [4096], P('tp'), may hold values from 0.5 to 6
- post_gain: float32 [4096], P('tp'), may hold values from 0.5 to 1.5
- lengths: int32 [4], replicated, may hold values from 1 to 1024, 3072 in all
Outputs:
- hidden_out: bfloat16 [4, 1024, 4096], P(None, 'seq', 'tp')
- new_out: bfloat16 [4, 4096], P(None, 'tp')
The draws below stay inside these ranges and needn't reach their ends.
Inputs may be any that keep to these rules, and one draw needn't show every extreme that they name: `lengths`: one prompt has exactly 1024 live tokens.
All inputs are finite; a program needn't handle non-finite values.
Results may differ from the reference program's by a relative error of at most 0.012.
The reference program's roundings to bfloat16 on the way (of `value` and `attention`) count: a program that leaves them out, or rounds other values in their place, can miss the bound.
Values may be sent and summed in bfloat16 or wider, within the bound.
A program may use at most 128 MiB of HBM per device.

```python
import math
import jax
import jax.numpy as jnp
import numpy as np
from jax import lax

D = 4096
HEADS = 32
HD = 128
SEQS = 4
LEN = 1024


def column_scale(size):
    return 0.5 + 1.5 * jnp.arange(size, dtype=jnp.float32) / size


def weight_base(key, shape):
    base = jax.random.normal(key, shape, jnp.float32)
    return base


def draw_w_qkv(key, part):
    base = weight_base(jax.random.fold_in(key, 11), (3, D, D))
    return (base * D ** (-0.5) * column_scale(D)).astype(jnp.bfloat16)


def draw_w_out(key, part):
    base = weight_base(jax.random.fold_in(key, 23), (D, D))
    return (base * D ** (-0.5) * column_scale(D)).astype(jnp.bfloat16)


def gain_draw(key, salt):
    uniform_part = jax.random.uniform(jax.random.fold_in(key, salt), (D,), jnp.float32)
    lower, upper = (0.5, 2.0)
    return jnp.exp(math.log(lower) + uniform_part * (math.log(upper) - math.log(lower)))


def draw_q_gain(key, part):
    return gain_draw(key, 37)


def draw_k_gain(key, part):
    return gain_draw(key, 41)


def steps_of(stream_key, extent, shards, least, largest):
    def one(dim, blocks):
        draws = jax.random.uniform(jax.random.fold_in(jax.random.fold_in(stream_key, 6), dim), (blocks,), jnp.float32, least / len(shards), largest / len(shards))
        return jnp.repeat(jnp.exp(draws), extent[dim] // blocks).reshape((-1,) + (1,) * (len(extent) - dim - 1))

    factor_of = one(*shards[0])
    for cut in shards[1:]:
        factor_of = factor_of * one(*cut)
    return factor_of


def length_profile(number_of, total, bound, skew):
    loads = [(1 << 20) // math.isqrt(rank ** skew) + 1 for rank in range(2, number_of + 1)]
    rest, counts = total - bound - (number_of - 1), [1] * (number_of - 1)
    while rest > 0:
        free = [i for i in range(number_of - 1) if counts[i] < bound]
        mass, left = sum([loads[i] for i in free]), rest
        for i in free:
            extra = min(bound - counts[i], max(1, left * loads[i] // mass), rest)
            counts[i] = counts[i] + extra
            rest = rest - extra
    return np.array([bound] + counts)


def uneven_parts(stream_key, number_of, total, most, slope):
    if number_of == 2:
        one = jax.random.randint(stream_key, (), max(1, total - most), min(most, total - 1) + 1)
        return jnp.stack([one, total - one])
    tallies = jnp.asarray(length_profile(number_of, total, most, slope), jnp.int32)
    couples = (number_of - 1) // 2
    giver, sink = tallies[1:1 + 2 * couples:2], tallies[2:2 + 2 * couples:2]
    room = jnp.minimum(giver - 1, most - sink)
    moved = jax.random.randint(jax.random.fold_in(stream_key, 1), (couples,), 0, 1 << 20) % (room + 1)
    tallies = tallies.at[1:1 + 2 * couples:2].set(giver - moved).at[2:2 + 2 * couples:2].set(sink + moved)
    return tallies[jax.random.permutation(jax.random.fold_in(stream_key, 2), number_of)]


def noise(rng, shape, scale, limit, pieces=(), held_as=jnp.bfloat16):
    values = jax.random.normal(rng, shape, jnp.float32) * scale
    if len(pieces) > 0:
        values = steps_of(rng, shape, pieces, -0.22, 0.18) * values
    return jnp.clip(values, min=-limit, max=limit).astype(held_as)


def setup_inputs(seed: int = 0) -> dict:
    seeds = jax.random.split(jax.random.key(seed), 9)
    return {
        "tokens": noise(seeds[0], (SEQS, LEN, D), 1.0, 6.0, ((1, 8), (2, 4))),
        "new_tokens": noise(seeds[1], (SEQS, D), 1.0, 6.0, ((1, 4),)),
        "w_qkv": draw_w_qkv(jax.random.fold_in(seeds[8], 71), 0),
        "w_out": draw_w_out(jax.random.fold_in(seeds[8], 71), 0),
        "q_gain": draw_q_gain(jax.random.fold_in(seeds[8], 71), 0),
        "k_gain": draw_k_gain(jax.random.fold_in(seeds[8], 71), 0),
        "post_gain": jnp.clip(1.0 + 0.1 * jax.random.normal(seeds[6], (D,), jnp.float32), 0.5, 1.5),
        "lengths": uneven_parts(seeds[7], SEQS, 3 * LEN, LEN, 1).astype(jnp.int32),
    }


rope_base = 500000.0
norm_eps = 1e-06
masked_fill = -1e+30

def rotate(values, position):
    half = values.shape[-1] // 2
    freq = rope_base ** (-(jnp.arange(half, dtype=jnp.float32) * 2.0) / values.shape[-1])
    angle = position.astype(jnp.float32)[..., None] * freq
    cosine = jnp.cos(angle)
    sine = jnp.sin(angle)
    lower = values[..., :half]
    upper = values[..., half:]
    return jnp.concatenate([lower * cosine - upper * sine, upper * cosine + lower * sine], -1)

def rms_scaled(values, gain):
    return values * lax.rsqrt(lax.optimization_barrier(jnp.mean(values * values, -1, keepdims=True)) + norm_eps) * gain

def attend_one(item):
    query_all, key_all, value_all, query_new, key_new, value_new, length = item
    scale = HD ** (-0.5)
    scores = jnp.dot(query_all, key_all.T, preferred_element_type=jnp.float32) * scale
    query_pos = jnp.arange(LEN, dtype=jnp.int32)[:, None]
    key_pos = jnp.arange(LEN, dtype=jnp.int32)[None, :]
    valid = (key_pos <= query_pos) & (key_pos < length)
    scores = jnp.where(valid, scores, masked_fill)
    top = lax.optimization_barrier(jnp.max(scores, -1, keepdims=True))
    weights = jnp.where(valid, jnp.exp(scores - top), 0.0)
    total = lax.optimization_barrier(jnp.sum(weights, -1, keepdims=True))
    prompt_out = jnp.dot(weights.astype(jnp.bfloat16), value_all, preferred_element_type=jnp.float32) / total
    new_scores = jnp.dot(key_all, query_new, preferred_element_type=jnp.float32) * scale
    live = jnp.arange(LEN, dtype=jnp.int32) < length
    new_scores = jnp.where(live, new_scores, masked_fill)
    self_score = jnp.dot(query_new, key_new, preferred_element_type=jnp.float32) * scale
    new_top = jnp.maximum(jnp.max(new_scores), self_score)
    new_weights = jnp.where(live, jnp.exp(new_scores - new_top), 0.0)
    own_weight = jnp.exp(self_score - new_top)
    new_total = jnp.sum(new_weights) + own_weight
    own_rounded = lax.optimization_barrier(own_weight.astype(jnp.bfloat16)).astype(jnp.float32)
    numer = jnp.dot(new_weights.astype(jnp.bfloat16), value_all, preferred_element_type=jnp.float32)
    numer = numer + own_rounded * value_new.astype(jnp.float32)
    return (prompt_out.astype(jnp.bfloat16), (numer / new_total).astype(jnp.bfloat16))

def reference(tokens, new_tokens, w_qkv, w_out, q_gain, k_gain, post_gain, lengths):
    prompt_rows = SEQS * LEN
    rows = jnp.concatenate([tokens.reshape(prompt_rows, D), new_tokens], 0)
    query_raw = jnp.dot(rows, w_qkv[0], preferred_element_type=jnp.float32)
    key_raw = jnp.dot(rows, w_qkv[1], preferred_element_type=jnp.float32)
    value = jnp.dot(rows, w_qkv[2], preferred_element_type=jnp.float32).astype(jnp.bfloat16)
    position = jnp.concatenate([jnp.tile(jnp.arange(LEN, dtype=jnp.int32), SEQS), lengths.astype(jnp.int32)], 0)
    query = rotate(rms_scaled(query_raw, q_gain).reshape(-1, HEADS, HD), position[:, None]).astype(jnp.bfloat16)
    key = rotate(rms_scaled(key_raw, k_gain).reshape(-1, HEADS, HD), position[:, None]).astype(jnp.bfloat16)
    value = value.reshape(-1, HEADS, HD)

    def by_head(array):
        return array[:prompt_rows].reshape(SEQS, LEN, HEADS, HD).transpose(0, 2, 1, 3).reshape(SEQS * HEADS, LEN, HD)

    def new_head(array):
        return array[prompt_rows:].reshape(SEQS * HEADS, HD)
    head_lengths = jnp.repeat(lengths.astype(jnp.int32), HEADS)
    prompt_attn, new_attn = lax.map(attend_one, (by_head(query), by_head(key), by_head(value), new_head(query), new_head(key), new_head(value), head_lengths))
    prompt_attn = prompt_attn.reshape(SEQS, HEADS, LEN, HD).transpose(0, 2, 1, 3).reshape(prompt_rows, D)
    new_attn = new_attn.reshape(SEQS, D)
    attention = jnp.concatenate([prompt_attn, new_attn], 0)
    projected = jnp.dot(attention, w_out, preferred_element_type=jnp.float32)
    result = (rows.astype(jnp.float32) + rms_scaled(projected, post_gain)).astype(jnp.bfloat16)
    return (result[:prompt_rows].reshape(SEQS, LEN, D), result[prompt_rows:])
```

```python
import jax
import jax.numpy as jnp
from jax import lax
from jax.sharding import PartitionSpec as P

HD = 128
PAD = 16
FAR = 1 << 30

rope_base = 500000.0
norm_eps = 1e-06
masked_fill = -1e30


def rope_tables(position):
    half = HD // 2
    freq = rope_base ** (-(jnp.arange(half, dtype=jnp.float32) * 2.0) / HD)
    angle = position.astype(jnp.float32)[:, None] * freq
    return jnp.cos(angle), jnp.sin(angle)


def rotate(values, cosine, sine):
    half = HD // 2
    lower = values[..., :half]
    upper = values[..., half:]
    return jnp.concatenate([lower * cosine - upper * sine, upper * cosine + lower * sine], -1)


def body(tokens, new_tokens, w_qkv, w_out, q_gain, k_gain, post_gain, lengths):
    seqs, pos_dev, width = tokens.shape
    heads = width // HD
    full = w_qkv.shape[1]
    shards = lax.axis_size("seq")
    group = shards // seqs
    piece = pos_dev // group
    me = lax.axis_index("seq")
    prompt, member = me // group, me % group
    count = shards * piece

    swapped = lax.all_to_all(tokens.reshape(shards, piece, width), "seq", 0, 0, tiled=True)
    fresh = lax.dynamic_slice_in_dim(new_tokens, prompt, 1, 0)
    rows = jnp.concatenate(
        [swapped.reshape(count, width), fresh, jnp.zeros((PAD - 1, width), tokens.dtype)], 0
    )
    everything = lax.all_gather(rows, "tp", axis=1, tiled=True)
    total = count + PAD
    proj = jnp.einsum("tn,cnf->ctf", everything, w_qkv, preferred_element_type=jnp.float32)
    squares = lax.psum(jnp.sum(proj[:2] * proj[:2], -1), "tp")
    factor = lax.rsqrt(squares / full + norm_eps)[..., None]

    length = lax.dynamic_index_in_dim(lengths, prompt, 0, keepdims=False)
    index = jnp.arange(count, dtype=jnp.int32)

    def positions(who):
        return (index // piece) * pos_dev + who * piece + index % piece

    tail = jnp.arange(PAD, dtype=jnp.int32) == 0
    position = jnp.concatenate([positions(member), jnp.where(tail, length, 0)])
    cosine, sine = rope_tables(position)
    cosine, sine = cosine[:, None], sine[:, None]

    def rotated(which, gain):
        normed = (proj[which] * factor[which] * gain).reshape(total, heads, HD)
        return rotate(normed, cosine, sine).astype(jnp.bfloat16)

    queries = rotated(0, q_gain)
    keys = rotated(1, k_gain)
    values = proj[2].astype(jnp.bfloat16).reshape(total, heads, HD)
    groups = [[b * group + g for g in range(group)] for b in range(seqs)]
    both = jnp.stack([keys[:count], values[:count]])
    gathered = lax.all_gather(both, "seq", axis=1, tiled=True, axis_index_groups=groups)
    all_keys = jnp.concatenate([gathered[0], keys[count:]], 0)
    all_values = jnp.concatenate([gathered[1], values[count:]], 0)
    key_pos = jnp.concatenate(
        [positions(g) for g in range(group)]
    )
    key_pos = jnp.concatenate([jnp.where(key_pos < length, key_pos, FAR + 1), jnp.where(tail, FAR, FAR + 1)])
    query_pos = jnp.concatenate([positions(member), jnp.where(tail, FAR, 0)])
    scores = jnp.einsum("phe,nhe->hpn", queries, all_keys, preferred_element_type=jnp.float32) * (
        HD ** (-0.5)
    )
    valid = (key_pos[None, :] <= query_pos[:, None])[None]
    scores = jnp.where(valid, scores, masked_fill)
    top = jnp.max(scores, -1, keepdims=True)
    weights = jnp.where(valid, jnp.exp(scores - top), 0.0)
    norm = jnp.sum(weights, -1)
    acc = jnp.einsum(
        "hpn,nhe->hpe", weights.astype(jnp.bfloat16), all_values, preferred_element_type=jnp.float32
    )
    attention = (acc / norm[..., None]).transpose(1, 0, 2).reshape(total, width).astype(jnp.bfloat16)

    part = jnp.dot(attention, w_out, preferred_element_type=jnp.float32).astype(jnp.bfloat16)
    own = lax.psum_scatter(part, "tp", scatter_dimension=1, tiled=True).astype(jnp.float32)
    mean = lax.psum(jnp.sum(own * own, -1), "tp") / full
    result = rows.astype(jnp.float32) + own * lax.rsqrt(mean[:, None] + norm_eps) * post_gain
    result = result.astype(jnp.bfloat16)
    out = lax.all_to_all(result[:count].reshape(shards, piece, width), "seq", 0, 0, tiled=True)
    new = lax.all_gather(result[count], "seq", axis=0)
    new = new.reshape(seqs, group, width)[:, 0]
    return out.reshape(seqs, pos_dev, width), new


def solution(mesh):
    in_specs = (
        P(None, "seq", "tp"),
        P(None, "tp"),
        P(None, None, "tp"),
        P("tp", None),
        P("tp"),
        P("tp"),
        P("tp"),
        P(),
    )
    out_specs = (P(None, "seq", "tp"), P(None, "tp"))
    return jax.shard_map(body, mesh=mesh, in_specs=in_specs, out_specs=out_specs, check_vma=False)
```

```python
from functools import partial

import jax
import jax.numpy as jnp
from jax import lax
from jax.experimental import pallas as pl
from jax.experimental.pallas import tpu as pltpu
from jax.sharding import PartitionSpec as P

HD = 128
PAD = 16
FAR = 1 << 30

rope_base = 500000.0
norm_eps = 1e-06
masked_fill = -1e30


def rope_tables(position):
    half = HD // 2
    freq = rope_base ** (-(jnp.arange(half, dtype=jnp.float32) * 2.0) / HD)
    angle = position.astype(jnp.float32)[:, None] * freq
    return jnp.cos(angle), jnp.sin(angle)


def rotate(values, cosine, sine):
    half = HD // 2
    lower = values[..., :half]
    upper = values[..., half:]
    return jnp.concatenate([lower * cosine - upper * sine, upper * cosine + lower * sine], -1)


def body(tokens, new_tokens, w_qkv, w_out, q_gain, k_gain, post_gain, lengths):
    seqs, pos_dev, width = tokens.shape
    heads = width // HD
    full = w_qkv.shape[1]
    shards = lax.axis_size("seq")
    group = shards // seqs
    piece = pos_dev // group
    me = lax.axis_index("seq")
    prompt, member = me // group, me % group
    count = shards * piece

    swapped = lax.all_to_all(tokens.reshape(shards, piece, width), "seq", 0, 0, tiled=True)
    fresh = lax.dynamic_slice_in_dim(new_tokens, prompt, 1, 0)
    rows = jnp.concatenate(
        [swapped.reshape(count, width), fresh, jnp.zeros((PAD - 1, width), tokens.dtype)], 0
    )
    everything = lax.all_gather(rows, "tp", axis=1, tiled=True)
    total = count + PAD
    proj = jnp.einsum("tn,cnf->ctf", everything, w_qkv, preferred_element_type=jnp.float32)
    squares = lax.psum(jnp.sum(proj[:2] * proj[:2], -1), "tp")
    factor = lax.rsqrt(squares / full + norm_eps)[..., None]

    length = lax.dynamic_index_in_dim(lengths, prompt, 0, keepdims=False)
    index = jnp.arange(count, dtype=jnp.int32)

    def positions(who):
        return (index // piece) * pos_dev + who * piece + index % piece

    tail = jnp.arange(PAD, dtype=jnp.int32) == 0
    position = jnp.concatenate([positions(member), jnp.where(tail, length, 0)])
    cosine, sine = rope_tables(position)
    cosine, sine = cosine[:, None], sine[:, None]

    def rotated(which, gain):
        normed = (proj[which] * factor[which] * gain).reshape(total, heads, HD)
        return rotate(normed, cosine, sine).astype(jnp.bfloat16)

    queries = rotated(0, q_gain)
    keys = rotated(1, k_gain)
    values = proj[2].astype(jnp.bfloat16).reshape(total, heads, HD)
    groups = [[b * group + g for g in range(group)] for b in range(seqs)]
    both = jnp.stack([keys[:count], values[:count]])
    gathered = lax.all_gather(both, "seq", axis=1, tiled=True, axis_index_groups=groups)
    all_keys = jnp.concatenate([gathered[0], keys[count:]], 0)
    all_values = jnp.concatenate([gathered[1], values[count:]], 0)
    key_pos = jnp.concatenate(
        [positions(g) for g in range(group)]
    )
    key_pos = jnp.concatenate([jnp.where(key_pos < length, key_pos, FAR + 1), jnp.where(tail, FAR, FAR + 1)])
    query_pos = jnp.concatenate([positions(member), jnp.where(tail, FAR, 0)])
    scores = jnp.einsum("phe,nhe->hpn", queries, all_keys, preferred_element_type=jnp.float32) * (
        HD ** (-0.5)
    )
    valid = (key_pos[None, :] <= query_pos[:, None])[None]
    scores = jnp.where(valid, scores, masked_fill)
    top = jnp.max(scores, -1, keepdims=True)
    weights = jnp.where(valid, jnp.exp(scores - top), 0.0)
    norm = jnp.sum(weights, -1)
    acc = jnp.einsum(
        "hpn,nhe->hpe", weights.astype(jnp.bfloat16), all_values, preferred_element_type=jnp.float32
    )
    attention = (acc / norm[..., None]).transpose(1, 0, 2).reshape(total, width).astype(jnp.bfloat16)

    part = jnp.dot(attention, w_out, preferred_element_type=jnp.float32).astype(jnp.bfloat16)
    own = lax.psum_scatter(part, "tp", scatter_dimension=1, tiled=True).astype(jnp.float32)
    mean = lax.psum(jnp.sum(own * own, -1), "tp") / full
    result = rows.astype(jnp.float32) + own * lax.rsqrt(mean[:, None] + norm_eps) * post_gain
    result = result.astype(jnp.bfloat16)
    out = lax.all_to_all(result[:count].reshape(shards, piece, width), "seq", 0, 0, tiled=True)
    new = lax.all_gather(result[count], "seq", axis=0)
    new = new.reshape(seqs, group, width)[:, 0]
    return out.reshape(seqs, pos_dev, width), new


MESH = pl.DeviceIdType.MESH
VMEM_LIMIT = 60 << 20
ROWS = 128


def remote(src, dst, send, recv, target):
    return pltpu.make_async_remote_copy(
        src_ref=src, dst_ref=dst, send_sem=send, recv_sem=recv, device_id=target, device_id_type=MESH
    )


def greet(targets):
    barrier = pltpu.get_barrier_semaphore()
    for target in targets:
        pl.semaphore_signal(barrier, inc=1, device_id=target, device_id_type=MESH)
    pl.semaphore_wait(barrier, len(targets))


def gather_project(shards, piece, tok, new, w, rows, raw, value, x, wv, acc, w_sem, loc_sem, a_send, a_recv, g_send, g_recv, n_send, n_recv):
    me, t = lax.axis_index("seq"), lax.axis_index("tp")
    width = tok.shape[2]
    count = shards * piece
    half = piece // 2
    near = [{"tp": t ^ j} for j in range(1, 4)]
    loads = []
    for j in range(4):
        load = pltpu.make_async_copy(w.at[:, pl.ds((t ^ j) * width, width), :], wv.at[j], w_sem.at[j])
        load.start()
        loads.append(load)
    own = pltpu.make_async_copy(tok.at[me], x.at[0, pl.ds(0, piece)], loc_sem.at[0])
    own.start()
    fresh = pltpu.make_async_copy(new, x.at[0, pl.ds(count, PAD)], loc_sem.at[1])
    fresh.start()
    greet([{"seq": me ^ k} for k in range(1, shards)] + near)

    swaps = []
    for k in range(1, shards):
        copy = remote(tok.at[me ^ k], x.at[0, pl.ds(k * piece, piece)], a_send.at[k], a_recv.at[k], {"seq": me ^ k})
        copy.start()
        swaps.append(copy)

    def first(j, k):
        at = x.at[0, pl.ds(k * piece, piece)]
        return remote(at, x.at[j, pl.ds(k * piece, piece)], g_send.at[j - 1, k], g_recv.at[j - 1, k], near[j - 1])

    def second(j, k):
        start = k * piece + (j - 1) * half
        return remote(
            x.at[j, pl.ds(start, half)], x.at[3, pl.ds(start, half)],
            g_send.at[1 + j, k], g_recv.at[1 + j, k], near[2 - j],
        )

    def tail(j):
        at = x.at[0, pl.ds(count, PAD)]
        return remote(at, x.at[j, pl.ds(count, PAD)], n_send.at[j - 1], n_recv.at[j - 1], near[j - 1])

    def multiply(j, start, size, clear):
        def tile(i, carry):
            c, col = i // 2, pl.ds(pl.multiple_of((i % 2) * (width // 2), width // 2), width // 2)
            part = jnp.dot(x[j, pl.ds(start, size), :], wv[j, c, :, col], preferred_element_type=jnp.float32)
            if clear:
                acc[c, pl.ds(start, size), col] = part
            else:
                acc[c, pl.ds(start, size), col] += part
            return carry

        lax.fori_loop(0, 6, tile, 0)

    def arrive(k):
        if k == 0:
            own.wait()
        else:
            swaps[k - 1].wait_recv()
        first(1, k).start()
        first(2, k).start()

    def forward(k):
        first(1, k).wait_recv()
        second(1, k).start()
        first(2, k).wait_recv()
        second(2, k).start()

    middle = shards // 2
    low, high = middle * piece, count - middle * piece + PAD
    for k in range(shards):
        arrive(k)
        if k == 0:
            fresh.wait()
            for j in range(1, 4):
                tail(j).start()
        if k >= 1:
            forward(k - 1)
        if k == middle:
            loads[0].wait()
            multiply(0, 0, low, True)
        if k == middle + 1:
            loads[1].wait()
            multiply(1, 0, low, False)
        if k == middle + 2:
            loads[2].wait()
            multiply(2, 0, low, False)
    forward(shards - 1)
    multiply(0, low, high, True)
    loads[3].wait()
    for k in range(middle):
        second(1, k).wait_recv()
        second(2, k).wait_recv()
    multiply(3, 0, low, False)
    for j in range(1, 4):
        tail(j).wait_recv()
    multiply(1, low, high, False)
    multiply(2, low, high, False)
    for k in range(middle, shards):
        second(1, k).wait_recv()
        second(2, k).wait_recv()
    multiply(3, low, high, False)
    raw[...] = acc[0:2]
    value[...] = acc[2].astype(jnp.bfloat16)
    rows[...] = x[0]
    for copy in swaps:
        copy.wait_send()
    for k in range(shards):
        for j in (1, 2):
            first(j, k).wait_send()
            second(j, k).wait_send()
    for j in range(1, 4):
        tail(j).wait_send()


def flat_tile(column):
    size = column.shape[0]
    wide = jnp.broadcast_to(column, (size, ROWS))
    if size < ROWS:
        wide = jnp.concatenate([wide, jnp.zeros((ROWS - size, ROWS), jnp.float32)], 0)
    return wide.T[0:8]


def tall_tile(flat, size):
    return jnp.broadcast_to(flat[0:1], (ROWS, ROWS)).T[0:size]


def lanes(block):
    total = block[:, 0:HD]
    for h in range(1, block.shape[1] // HD):
        total = total + block[:, h * HD : (h + 1) * HD]
    return total


def attend(full, raw, value, cos, sin, qpos, kpos, qg, kg, out, sq, sq_in, q, ka, va, bias, s_send, s_recv, p_send, p_recv, loc_sem):
    me, t = lax.axis_index("seq"), lax.axis_index("tp")
    total, width = value.shape
    count = total - PAD
    heads = width // HD
    near = [{"tp": t ^ j} for j in range(1, 4)]
    mate = {"seq": me ^ 1}
    spans = [(i * ROWS, ROWS) for i in range(count // ROWS)] + [(count, PAD)]
    tiles = len(spans)
    greet(near + [mate])
    send_v = remote(value.at[pl.ds(0, count)], va.at[pl.ds(count, count)], p_send.at[0], p_recv.at[0], mate)
    send_v.start()
    for which in range(2):
        for i, (start, size) in enumerate(spans):
            block = raw[which, start : start + size, :]
            column = jnp.sum(lanes(block * block), -1, keepdims=True)
            sq[which * tiles + i] = flat_tile(column)
    squares = [remote(sq, sq_in.at[j], s_send.at[j], s_recv.at[j], near[j]) for j in range(3)]
    for copy in squares:
        copy.start()
    va[0:count, :] = value[0:count, :]
    va[2 * count :, :] = value[count:, :]
    for start, size in spans:
        bias[start : start + size, :] = jnp.where(kpos[...] <= qpos[start : start + size, :], 0.0, masked_fill)
    for copy in squares:
        copy.wait_recv()

    def finish(which, gain, start, size, i):
        slot = which * tiles + i
        flat = sq[slot] + sq_in[0, slot] + sq_in[1, slot] + sq_in[2, slot]
        factor = lax.rsqrt(tall_tile(flat, size) / full + norm_eps)
        c, s = cos[start : start + size, :], sin[start : start + size, :]
        parts = []
        for h in range(heads):
            at = slice(h * HD, (h + 1) * HD)
            normed = raw[which, start : start + size, at] * factor * gain[:, at]
            parts.append((normed * c + pltpu.roll(normed, HD // 2, 1) * s).astype(jnp.bfloat16))
        return jnp.concatenate(parts, -1)

    for i, (start, size) in enumerate(spans):
        place = start if start < count else 2 * count
        ka[place : place + size, :] = finish(1, kg, start, size, i)
    send_k = remote(ka.at[pl.ds(0, count)], ka.at[pl.ds(count, count)], p_send.at[1], p_recv.at[1], mate)
    send_k.start()
    for i, (start, size) in enumerate(spans):
        q[start : start + size, :] = finish(0, qg, start, size, i)
    send_v.wait_recv()
    send_k.wait_recv()

    def one_head(h, carry):
        at = pl.ds(pl.multiple_of(h * HD, HD), HD)
        for start, size in spans:
            scores = lax.dot_general(
                q[start : start + size, at], ka[:, at], (((1,), (1,)), ((), ())), preferred_element_type=jnp.float32
            )
            scores = scores + bias[start : start + size, :]
            top = jnp.max(scores, -1, keepdims=True)
            weights = jnp.exp((scores - top) * (HD ** (-0.5)))
            norm = jnp.sum(weights, -1, keepdims=True)
            mixed = jnp.dot(weights.astype(jnp.bfloat16), va[:, at], preferred_element_type=jnp.float32)
            out[start : start + size, at] = (mixed / norm).astype(jnp.bfloat16)
        return carry

    lax.fori_loop(0, heads, one_head, 0)
    for copy in squares:
        copy.wait_send()
    send_v.wait_send()
    send_k.wait_send()


def in_vmem():
    return pl.BlockSpec(memory_space=pltpu.VMEM)


def call_gather(tokens, new, w_qkv, shards, piece):
    width = tokens.shape[2]
    total = shards * piece + PAD
    dma = pltpu.SemaphoreType.DMA
    return pl.pallas_call(
        partial(gather_project, shards, piece),
        out_shape=(
            jax.ShapeDtypeStruct((total, width), jnp.bfloat16),
            jax.ShapeDtypeStruct((2, total, width), jnp.float32),
            jax.ShapeDtypeStruct((total, width), jnp.bfloat16),
        ),
        in_specs=[in_vmem(), in_vmem(), pl.BlockSpec(memory_space=pl.ANY)],
        out_specs=(in_vmem(), in_vmem(), in_vmem()),
        scratch_shapes=[
            pltpu.VMEM((4, total, width), jnp.bfloat16),
            pltpu.VMEM((4, 3, width, width), jnp.bfloat16),
            pltpu.VMEM((3, total, width), jnp.float32),
            dma((4,)),
            dma((2,)),
            dma((shards,)),
            dma((shards,)),
            dma((4, shards)),
            dma((4, shards)),
            dma((3,)),
            dma((3,)),
        ],
        compiler_params=pltpu.CompilerParams(collective_id=0, has_side_effects=True, vmem_limit_bytes=VMEM_LIMIT),
        name="gather_project",
    )(tokens, new, w_qkv)


def call_attend(full, raw, value, cos, sin, qpos, kpos, qg, kg):
    total, width = value.shape
    keys = 2 * (total - PAD) + PAD
    tiles = (total - PAD) // ROWS + 1
    dma = pltpu.SemaphoreType.DMA
    return pl.pallas_call(
        partial(attend, full),
        out_shape=jax.ShapeDtypeStruct((total, width), jnp.bfloat16),
        in_specs=[in_vmem()] * 8,
        out_specs=in_vmem(),
        scratch_shapes=[
            pltpu.VMEM((2 * tiles, 8, ROWS), jnp.float32),
            pltpu.VMEM((3, 2 * tiles, 8, ROWS), jnp.float32),
            pltpu.VMEM((total, width), jnp.bfloat16),
            pltpu.VMEM((keys, width), jnp.bfloat16),
            pltpu.VMEM((keys, width), jnp.bfloat16),
            pltpu.VMEM((total, keys), jnp.float32),
            dma((3,)),
            dma((3,)),
            dma((2,)),
            dma((2,)),
            dma((1,)),
        ],
        compiler_params=pltpu.CompilerParams(collective_id=1, has_side_effects=True, vmem_limit_bytes=VMEM_LIMIT),
        name="attend",
    )(raw, value, cos, sin, qpos, kpos, qg, kg)


def fast_body(tokens, new_tokens, w_qkv, w_out, q_gain, k_gain, post_gain, lengths):
    seqs, pos_dev, width = tokens.shape
    full = w_qkv.shape[1]
    shards = lax.axis_size("seq")
    group = shards // seqs
    piece = pos_dev // group
    me = lax.axis_index("seq")
    prompt, member = me // group, me % group
    count = shards * piece
    fresh = lax.dynamic_slice_in_dim(new_tokens, prompt, 1, 0)
    fresh = jnp.pad(fresh, ((0, PAD - 1), (0, 0)))
    rows, raw, value = call_gather(tokens.reshape(shards, piece, width), fresh, w_qkv, shards, piece)

    length = lax.dynamic_index_in_dim(lengths, prompt, 0, keepdims=False)
    index = jnp.arange(count, dtype=jnp.int32)

    def positions(who):
        return ((index // piece) ^ who) * pos_dev + (who % group) * piece + index % piece

    tail = jnp.arange(PAD, dtype=jnp.int32) == 0
    position = jnp.concatenate([positions(me), jnp.where(tail, length, 0)])
    cosine, sine = rope_tables(position)
    cos = jnp.concatenate([cosine, cosine], -1)
    sin = jnp.concatenate([-sine, sine], -1)
    key_pos = jnp.concatenate([positions(me), positions(me ^ 1)])
    key_pos = jnp.concatenate(
        [jnp.where(key_pos < length, key_pos, FAR + 1), jnp.where(tail, FAR, FAR + 1)]
    )
    query_pos = jnp.concatenate([positions(me), jnp.where(tail, FAR, 0)])
    attention = call_attend(
        full, raw, value, cos, sin, query_pos[:, None], key_pos[None, :], q_gain[None], k_gain[None]
    )
    return finish_fast(attention, w_out, rows, post_gain, full, seqs, pos_dev)


def finish_fast(attention, w_out, rows, post_gain, full, seqs, pos_dev):
    width = rows.shape[1]
    shards = lax.axis_size("seq")
    group = shards // seqs
    piece = pos_dev // group
    me = lax.axis_index("seq")
    count = shards * piece
    part = jnp.dot(attention, w_out, preferred_element_type=jnp.float32).astype(jnp.bfloat16)
    own = lax.psum_scatter(part, "tp", scatter_dimension=1, tiled=True).astype(jnp.float32)
    mean = lax.psum(jnp.sum(own * own, -1), "tp") / full
    result = rows.astype(jnp.float32) + own * lax.rsqrt(mean[:, None] + norm_eps) * post_gain
    result = result.astype(jnp.bfloat16)
    blocks = jnp.stack(
        [lax.dynamic_slice_in_dim(result, (me ^ k) * piece, piece, 0) for k in range(shards)]
    )
    out = lax.all_to_all(blocks, "seq", 0, 0, tiled=True)
    new = lax.all_gather(result[count], "seq", axis=0)
    new = new.reshape(seqs, group, width)[:, 0]
    return out.reshape(seqs, pos_dev, width), new


def solution(mesh):
    in_specs = (
        P(None, "seq", "tp"),
        P(None, "tp"),
        P(None, None, "tp"),
        P("tp", None),
        P("tp"),
        P("tp"),
        P("tp"),
        P(),
    )
    out_specs = (P(None, "seq", "tp"), P(None, "tp"))
    chosen = fast_body if (mesh.shape["seq"], mesh.shape["tp"]) == (8, 4) else body
    return jax.shard_map(chosen, mesh=mesh, in_specs=in_specs, out_specs=out_specs, check_vma=False)
```

```python
from functools import partial

import jax
import jax.numpy as jnp
from jax import lax
from jax.experimental import pallas as pl
from jax.experimental.pallas import tpu as pltpu
from jax.sharding import PartitionSpec as P

HD = 128
PAD = 16
FAR = 1 << 30

rope_base = 500000.0
norm_eps = 1e-06
masked_fill = -1e30


def rope_tables(position):
    half = HD // 2
    freq = rope_base ** (-(jnp.arange(half, dtype=jnp.float32) * 2.0) / HD)
    angle = position.astype(jnp.float32)[:, None] * freq
    return jnp.cos(angle), jnp.sin(angle)


def rotate(values, cosine, sine):
    half = HD // 2
    lower = values[..., :half]
    upper = values[..., half:]
    return jnp.concatenate([lower * cosine - upper * sine, upper * cosine + lower * sine], -1)


def body(tokens, new_tokens, w_qkv, w_out, q_gain, k_gain, post_gain, lengths):
    seqs, pos_dev, width = tokens.shape
    heads = width // HD
    full = w_qkv.shape[1]
    shards = lax.axis_size("seq")
    group = shards // seqs
    piece = pos_dev // group
    me = lax.axis_index("seq")
    prompt, member = me // group, me % group
    count = shards * piece

    swapped = lax.all_to_all(tokens.reshape(shards, piece, width), "seq", 0, 0, tiled=True)
    fresh = lax.dynamic_slice_in_dim(new_tokens, prompt, 1, 0)
    rows = jnp.concatenate(
        [swapped.reshape(count, width), fresh, jnp.zeros((PAD - 1, width), tokens.dtype)], 0
    )
    everything = lax.all_gather(rows, "tp", axis=1, tiled=True)
    total = count + PAD
    proj = jnp.einsum("tn,cnf->ctf", everything, w_qkv, preferred_element_type=jnp.float32)
    squares = lax.psum(jnp.sum(proj[:2] * proj[:2], -1), "tp")
    factor = lax.rsqrt(squares / full + norm_eps)[..., None]

    length = lax.dynamic_index_in_dim(lengths, prompt, 0, keepdims=False)
    index = jnp.arange(count, dtype=jnp.int32)

    def positions(who):
        return (index // piece) * pos_dev + who * piece + index % piece

    tail = jnp.arange(PAD, dtype=jnp.int32) == 0
    position = jnp.concatenate([positions(member), jnp.where(tail, length, 0)])
    cosine, sine = rope_tables(position)
    cosine, sine = cosine[:, None], sine[:, None]

    def rotated(which, gain):
        normed = (proj[which] * factor[which] * gain).reshape(total, heads, HD)
        return rotate(normed, cosine, sine).astype(jnp.bfloat16)

    queries = rotated(0, q_gain)
    keys = rotated(1, k_gain)
    values = proj[2].astype(jnp.bfloat16).reshape(total, heads, HD)
    groups = [[b * group + g for g in range(group)] for b in range(seqs)]
    both = jnp.stack([keys[:count], values[:count]])
    gathered = lax.all_gather(both, "seq", axis=1, tiled=True, axis_index_groups=groups)
    all_keys = jnp.concatenate([gathered[0], keys[count:]], 0)
    all_values = jnp.concatenate([gathered[1], values[count:]], 0)
    key_pos = jnp.concatenate(
        [positions(g) for g in range(group)]
    )
    key_pos = jnp.concatenate([jnp.where(key_pos < length, key_pos, FAR + 1), jnp.where(tail, FAR, FAR + 1)])
    query_pos = jnp.concatenate([positions(member), jnp.where(tail, FAR, 0)])
    scores = jnp.einsum("phe,nhe->hpn", queries, all_keys, preferred_element_type=jnp.float32) * (
        HD ** (-0.5)
    )
    valid = (key_pos[None, :] <= query_pos[:, None])[None]
    scores = jnp.where(valid, scores, masked_fill)
    top = jnp.max(scores, -1, keepdims=True)
    weights = jnp.where(valid, jnp.exp(scores - top), 0.0)
    norm = jnp.sum(weights, -1)
    acc = jnp.einsum(
        "hpn,nhe->hpe", weights.astype(jnp.bfloat16), all_values, preferred_element_type=jnp.float32
    )
    attention = (acc / norm[..., None]).transpose(1, 0, 2).reshape(total, width).astype(jnp.bfloat16)

    part = jnp.dot(attention, w_out, preferred_element_type=jnp.float32).astype(jnp.bfloat16)
    own = lax.psum_scatter(part, "tp", scatter_dimension=1, tiled=True).astype(jnp.float32)
    mean = lax.psum(jnp.sum(own * own, -1), "tp") / full
    result = rows.astype(jnp.float32) + own * lax.rsqrt(mean[:, None] + norm_eps) * post_gain
    result = result.astype(jnp.bfloat16)
    out = lax.all_to_all(result[:count].reshape(shards, piece, width), "seq", 0, 0, tiled=True)
    new = lax.all_gather(result[count], "seq", axis=0)
    new = new.reshape(seqs, group, width)[:, 0]
    return out.reshape(seqs, pos_dev, width), new


MESH = pl.DeviceIdType.MESH
VMEM_LIMIT = 60 << 20
ROWS = 128


def remote(src, dst, send, recv, target):
    return pltpu.make_async_remote_copy(
        src_ref=src, dst_ref=dst, send_sem=send, recv_sem=recv, device_id=target, device_id_type=MESH
    )


def greet(targets):
    barrier = pltpu.get_barrier_semaphore()
    for target in targets:
        pl.semaphore_signal(barrier, inc=1, device_id=target, device_id_type=MESH)
    pl.semaphore_wait(barrier, len(targets))


def gather_project(shards, piece, tok, new, w, rows, raw, value, x, wv, acc, w_sem, loc_sem, a_send, a_recv, g_send, g_recv, n_send, n_recv):
    me, t = lax.axis_index("seq"), lax.axis_index("tp")
    width = tok.shape[2]
    count = shards * piece
    half = piece // 2
    near = [{"tp": t ^ j} for j in range(1, 4)]
    loads = []
    for j in range(4):
        load = pltpu.make_async_copy(w.at[:, pl.ds((t ^ j) * width, width), :], wv.at[j], w_sem.at[j])
        load.start()
        loads.append(load)
    own = pltpu.make_async_copy(tok.at[me], x.at[0, pl.ds(0, piece)], loc_sem.at[0])
    own.start()
    fresh = pltpu.make_async_copy(new, x.at[0, pl.ds(count, PAD)], loc_sem.at[1])
    fresh.start()
    greet([{"seq": me ^ k} for k in range(1, shards)] + near)

    swaps = []
    for k in range(1, shards):
        copy = remote(tok.at[me ^ k], x.at[0, pl.ds(k * piece, piece)], a_send.at[k], a_recv.at[k], {"seq": me ^ k})
        copy.start()
        swaps.append(copy)

    def first(j, k):
        at = x.at[0, pl.ds(k * piece, piece)]
        return remote(at, x.at[j, pl.ds(k * piece, piece)], g_send.at[j - 1, k], g_recv.at[j - 1, k], near[j - 1])

    def second(j, k):
        start = k * piece + (j - 1) * half
        return remote(
            x.at[j, pl.ds(start, half)], x.at[3, pl.ds(start, half)],
            g_send.at[1 + j, k], g_recv.at[1 + j, k], near[2 - j],
        )

    def tail(j):
        at = x.at[0, pl.ds(count, PAD)]
        return remote(at, x.at[j, pl.ds(count, PAD)], n_send.at[j - 1], n_recv.at[j - 1], near[j - 1])

    def multiply(j, start, size, clear):
        def tile(i, carry):
            c, col = i // 2, pl.ds(pl.multiple_of((i % 2) * (width // 2), width // 2), width // 2)
            part = jnp.dot(x[j, pl.ds(start, size), :], wv[j, c, :, col], preferred_element_type=jnp.float32)
            if clear:
                acc[c, pl.ds(start, size), col] = part
            else:
                acc[c, pl.ds(start, size), col] += part
            return carry

        lax.fori_loop(0, 6, tile, 0)

    def arrive(k):
        if k == 0:
            own.wait()
        else:
            swaps[k - 1].wait_recv()
        first(1, k).start()
        first(2, k).start()

    def forward(k):
        first(1, k).wait_recv()
        second(1, k).start()
        first(2, k).wait_recv()
        second(2, k).start()

    middle = shards // 2
    low, high = middle * piece, count - middle * piece + PAD
    for k in range(shards):
        arrive(k)
        if k == 0:
            fresh.wait()
            for j in range(1, 4):
                tail(j).start()
        if k >= 1:
            forward(k - 1)
        if k == middle:
            loads[0].wait()
            multiply(0, 0, low, True)
        if k == middle + 1:
            loads[1].wait()
            multiply(1, 0, low, False)
        if k == middle + 2:
            loads[2].wait()
            multiply(2, 0, low, False)
    forward(shards - 1)
    multiply(0, low, high, True)
    loads[3].wait()
    for k in range(middle):
        second(1, k).wait_recv()
        second(2, k).wait_recv()
    multiply(3, 0, low, False)
    for j in range(1, 4):
        tail(j).wait_recv()
    multiply(1, low, high, False)
    multiply(2, low, high, False)
    for k in range(middle, shards):
        second(1, k).wait_recv()
        second(2, k).wait_recv()
    multiply(3, low, high, False)
    raw[...] = acc[0:2]
    value[...] = acc[2].astype(jnp.bfloat16)
    rows[...] = x[0]
    for copy in swaps:
        copy.wait_send()
    for k in range(shards):
        for j in (1, 2):
            first(j, k).wait_send()
            second(j, k).wait_send()
    for j in range(1, 4):
        tail(j).wait_send()


def flat_tile(column):
    size = column.shape[0]
    wide = jnp.broadcast_to(column, (size, ROWS))
    if size < ROWS:
        wide = jnp.concatenate([wide, jnp.zeros((ROWS - size, ROWS), jnp.float32)], 0)
    return wide.T[0:8]


def tall_tile(flat, size):
    return jnp.broadcast_to(flat[0:1], (ROWS, ROWS)).T[0:size]


def lanes(block):
    total = block[:, 0:HD]
    for h in range(1, block.shape[1] // HD):
        total = total + block[:, h * HD : (h + 1) * HD]
    return total


def attend(full, raw, value, cos, sin, qpos, kpos, qg, kg, out, sq, sq_in, q, ka, va, bias, s_send, s_recv, p_send, p_recv, loc_sem):
    me, t = lax.axis_index("seq"), lax.axis_index("tp")
    total, width = value.shape
    count = total - PAD
    heads = width // HD
    near = [{"tp": t ^ j} for j in range(1, 4)]
    mate = {"seq": me ^ 1}
    spans = [(i * ROWS, ROWS) for i in range(count // ROWS)] + [(count, PAD)]
    tiles = len(spans)
    greet(near + [mate])
    send_v = remote(value.at[pl.ds(0, count)], va.at[pl.ds(count, count)], p_send.at[0], p_recv.at[0], mate)
    send_v.start()
    for which in range(2):
        for i, (start, size) in enumerate(spans):
            block = raw[which, start : start + size, :]
            column = jnp.sum(lanes(block * block), -1, keepdims=True)
            sq[which * tiles + i] = flat_tile(column)
    squares = [remote(sq, sq_in.at[j], s_send.at[j], s_recv.at[j], near[j]) for j in range(3)]
    for copy in squares:
        copy.start()
    va[0:count, :] = value[0:count, :]
    va[2 * count :, :] = value[count:, :]
    for start, size in spans:
        bias[start : start + size, :] = jnp.where(kpos[...] <= qpos[start : start + size, :], 0.0, masked_fill)
    for copy in squares:
        copy.wait_recv()

    def finish(which, gain, start, size, i):
        slot = which * tiles + i
        flat = sq[slot] + sq_in[0, slot] + sq_in[1, slot] + sq_in[2, slot]
        factor = lax.rsqrt(tall_tile(flat, size) / full + norm_eps)
        c, s = cos[start : start + size, :], sin[start : start + size, :]
        parts = []
        for h in range(heads):
            at = slice(h * HD, (h + 1) * HD)
            normed = raw[which, start : start + size, at] * factor * gain[:, at]
            parts.append((normed * c + pltpu.roll(normed, HD // 2, 1) * s).astype(jnp.bfloat16))
        return jnp.concatenate(parts, -1)

    for i, (start, size) in enumerate(spans):
        place = start if start < count else 2 * count
        ka[place : place + size, :] = finish(1, kg, start, size, i)
    send_k = remote(ka.at[pl.ds(0, count)], ka.at[pl.ds(count, count)], p_send.at[1], p_recv.at[1], mate)
    send_k.start()
    for i, (start, size) in enumerate(spans):
        q[start : start + size, :] = finish(0, qg, start, size, i)
    send_v.wait_recv()
    send_k.wait_recv()

    def one_head(h, carry):
        at = pl.ds(pl.multiple_of(h * HD, HD), HD)
        for start, size in spans:
            scores = lax.dot_general(
                q[start : start + size, at], ka[:, at], (((1,), (1,)), ((), ())), preferred_element_type=jnp.float32
            )
            scores = scores + bias[start : start + size, :]
            top = jnp.max(scores, -1, keepdims=True)
            weights = jnp.exp((scores - top) * (HD ** (-0.5)))
            norm = jnp.sum(weights, -1, keepdims=True)
            mixed = jnp.dot(weights.astype(jnp.bfloat16), va[:, at], preferred_element_type=jnp.float32)
            out[start : start + size, at] = (mixed / norm).astype(jnp.bfloat16)
        return carry

    lax.fori_loop(0, heads, one_head, 0)
    for copy in squares:
        copy.wait_send()
    send_v.wait_send()
    send_k.wait_send()


def in_vmem():
    return pl.BlockSpec(memory_space=pltpu.VMEM)


def call_gather(tokens, new, w_qkv, shards, piece):
    width = tokens.shape[2]
    total = shards * piece + PAD
    dma = pltpu.SemaphoreType.DMA
    return pl.pallas_call(
        partial(gather_project, shards, piece),
        out_shape=(
            jax.ShapeDtypeStruct((total, width), jnp.bfloat16),
            jax.ShapeDtypeStruct((2, total, width), jnp.float32),
            jax.ShapeDtypeStruct((total, width), jnp.bfloat16),
        ),
        in_specs=[in_vmem(), in_vmem(), pl.BlockSpec(memory_space=pl.ANY)],
        out_specs=(in_vmem(), in_vmem(), in_vmem()),
        scratch_shapes=[
            pltpu.VMEM((4, total, width), jnp.bfloat16),
            pltpu.VMEM((4, 3, width, width), jnp.bfloat16),
            pltpu.VMEM((3, total, width), jnp.float32),
            dma((4,)),
            dma((2,)),
            dma((shards,)),
            dma((shards,)),
            dma((4, shards)),
            dma((4, shards)),
            dma((3,)),
            dma((3,)),
        ],
        compiler_params=pltpu.CompilerParams(collective_id=0, has_side_effects=True, vmem_limit_bytes=VMEM_LIMIT),
        name="gather_project",
    )(tokens, new, w_qkv)


def call_attend(full, raw, value, cos, sin, qpos, kpos, qg, kg):
    total, width = value.shape
    keys = 2 * (total - PAD) + PAD
    tiles = (total - PAD) // ROWS + 1
    dma = pltpu.SemaphoreType.DMA
    return pl.pallas_call(
        partial(attend, full),
        out_shape=jax.ShapeDtypeStruct((total, width), jnp.bfloat16),
        in_specs=[in_vmem()] * 8,
        out_specs=in_vmem(),
        scratch_shapes=[
            pltpu.VMEM((2 * tiles, 8, ROWS), jnp.float32),
            pltpu.VMEM((3, 2 * tiles, 8, ROWS), jnp.float32),
            pltpu.VMEM((total, width), jnp.bfloat16),
            pltpu.VMEM((keys, width), jnp.bfloat16),
            pltpu.VMEM((keys, width), jnp.bfloat16),
            pltpu.VMEM((total, keys), jnp.float32),
            dma((3,)),
            dma((3,)),
            dma((2,)),
            dma((2,)),
            dma((1,)),
        ],
        compiler_params=pltpu.CompilerParams(collective_id=1, has_side_effects=True, vmem_limit_bytes=VMEM_LIMIT),
        name="attend",
    )(raw, value, cos, sin, qpos, kpos, qg, kg)


def project_return(full, shards, piece, group, att, w, rows, gain, out, new, wv, d3, r3, s1, s2, r1, r2, p0, p1, p2, o, sq, sq_in, w_sem, l_sem, d_send, d_recv, m_send, m_recv, s_send, s_recv, z_send, z_recv, n_send, n_recv):
    me, t = lax.axis_index("seq"), lax.axis_index("tp")
    total, width = att.shape
    count = total - PAD
    prompt = me // group
    near = [{"tp": t ^ j} for j in range(1, 4)]
    loads = []
    for j in range(4):
        loads.append(pltpu.make_async_copy(w.at[:, pl.ds((t ^ j) * width, width)], wv.at[j], w_sem.at[j]))
    for j in (3, 2, 1, 0):
        loads[j].start()
    greet([{"seq": me ^ k} for k in range(1, shards)] + near)
    split = count // 2
    side = ROWS // 2
    spans = [(start, side, side) for start in range(split, count, ROWS)] + [(count, PAD, 0)]
    late = len(spans)
    spans += [(start, side, side) for start in range(split - ROWS, -1, -ROWS)]

    def product(j, start, size, target):
        def tile(i, carry):
            col = pl.ds(pl.multiple_of(i * (width // 2), width // 2), width // 2)
            part = jnp.dot(att[pl.ds(start, size), :], wv[j, :, col], preferred_element_type=jnp.float32)
            target[pl.ds(start, size), col] = part.astype(target.dtype)
            return carry

        lax.fori_loop(0, 2, tile, 0)

    def diagonal(i):
        start, a, b = spans[i]
        copies = [remote(d3.at[pl.ds(start, a)], r3.at[pl.ds(start, a)], d_send.at[0, i], d_recv.at[0, i], near[0])]
        if b:
            copies.append(
                remote(d3.at[pl.ds(start + a, b)], r3.at[pl.ds(start + a, b)], d_send.at[1, i], d_recv.at[1, i], near[1])
            )
        return copies

    def merged(i):
        start, a, b = spans[i]
        at = pl.ds(start, a + b)
        return [
            remote(s2.at[at], r2.at[at], m_send.at[1, i], m_recv.at[1, i], near[1]),
            remote(s1.at[at], r1.at[at], m_send.at[0, i], m_recv.at[0, i], near[0]),
        ]

    def merge(i):
        start, a, b = spans[i]
        first, last = slice(start, start + a), slice(start + a, start + a + b)
        copies, sums = diagonal(i), merged(i)
        copies[0].wait_recv()
        s2[first, :] = (p2[first, :] + r3[first, :].astype(jnp.float32)).astype(jnp.bfloat16)
        if b:
            s2[last, :] = p2[last, :].astype(jnp.bfloat16)
        sums[0].start()
        s1[first, :] = p1[first, :].astype(jnp.bfloat16)
        if b:
            copies[1].wait_recv()
            s1[last, :] = (p1[last, :] + r3[last, :].astype(jnp.float32)).astype(jnp.bfloat16)
        sums[1].start()

    high = count - split + PAD
    loads[3].wait()
    product(3, split, high, d3)
    for i in range(late):
        for copy in diagonal(i):
            copy.start()
    product(3, 0, split, d3)
    for i in range(late, len(spans)):
        for copy in diagonal(i):
            copy.start()
    loads[2].wait()
    product(2, split, high, p2)
    loads[1].wait()
    product(1, split, high, p1)
    for i in range(late):
        merge(i)
    product(2, 0, split, p2)
    product(1, 0, split, p1)
    for i in range(late, len(spans)):
        merge(i)
    loads[0].wait()
    product(0, split, high, p0)
    product(0, 0, split, p0)

    def squares(i):
        return [remote(sq.at[i], sq_in.at[j, i], s_send.at[j, i], s_recv.at[j, i], near[j]) for j in range(3)]

    def swap(k):
        return remote(o.at[pl.ds(k * piece, piece)], out.at[me], z_send.at[k], z_recv.at[k], {"seq": me ^ k})

    def fresh(m):
        return remote(o.at[pl.ds(count, PAD)], new.at[prompt], n_send.at[m - 1], n_recv.at[m - 1], {"seq": me ^ (m * group)})

    local = pltpu.make_async_copy(o.at[pl.ds(0, piece)], out.at[me], l_sem.at[0])
    local_new = pltpu.make_async_copy(o.at[pl.ds(count, PAD)], new.at[prompt], l_sem.at[1])

    def stage_one(i):
        start, a, b = spans[i]
        at = slice(start, start + a + b)
        for copy in merged(i):
            copy.wait_recv()
        own = p0[at, :] + r1[at, :].astype(jnp.float32) + r2[at, :].astype(jnp.float32)
        p0[at, :] = own
        sq[i] = flat_tile(jnp.sum(lanes(own * own), -1, keepdims=True))
        for copy in squares(i):
            copy.start()

    def stage_two(i):
        start, a, b = spans[i]
        at = slice(start, start + a + b)
        for copy in squares(i):
            copy.wait_recv()
        flat = sq[i] + sq_in[0, i] + sq_in[1, i] + sq_in[2, i]
        factor = lax.rsqrt(tall_tile(flat, a + b) / full + norm_eps)
        for h in range(width // HD):
            col = slice(h * HD, (h + 1) * HD)
            o[at, col] = (
                rows[at, col].astype(jnp.float32) + p0[at, col] * factor * gain[:, col]
            ).astype(jnp.bfloat16)
        if start == count:
            local_new.start()
            for m in range(1, shards // group):
                fresh(m).start()
        else:
            for k in range(start // piece, (start + a + b) // piece):
                if k == 0:
                    local.start()
                else:
                    swap(k).start()

    for i in range(len(spans)):
        stage_one(i)
        if i >= 1:
            stage_two(i - 1)
    stage_two(len(spans) - 1)
    local.wait()
    local_new.wait()
    for k in range(1, shards):
        swap(k).wait()
    for m in range(1, shards // group):
        fresh(m).wait()
    for i in range(len(spans)):
        for copy in diagonal(i) + merged(i) + squares(i):
            copy.wait_send()


def call_project(full, shards, piece, group, attention, w_out, rows, gain):
    total, width = rows.shape
    seqs = shards // group
    tiles = (total - PAD) // ROWS + 1
    dma = pltpu.SemaphoreType.DMA
    half = pltpu.VMEM((total, width), jnp.bfloat16)
    wide = pltpu.VMEM((total, width), jnp.float32)
    return pl.pallas_call(
        partial(project_return, full, shards, piece, group),
        out_shape=(
            jax.ShapeDtypeStruct((shards, piece, width), jnp.bfloat16),
            jax.ShapeDtypeStruct((seqs, PAD, width), jnp.bfloat16),
        ),
        in_specs=[in_vmem(), pl.BlockSpec(memory_space=pl.ANY), in_vmem(), in_vmem()],
        out_specs=(in_vmem(), in_vmem()),
        scratch_shapes=[
            pltpu.VMEM((4, width, width), jnp.bfloat16),
            half, half, half, half, half, half,
            wide, wide, wide,
            half,
            pltpu.VMEM((tiles, 8, ROWS), jnp.float32),
            pltpu.VMEM((3, tiles, 8, ROWS), jnp.float32),
            dma((4,)),
            dma((2,)),
            dma((2, tiles)),
            dma((2, tiles)),
            dma((2, tiles)),
            dma((2, tiles)),
            dma((3, tiles)),
            dma((3, tiles)),
            dma((shards,)),
            dma((shards,)),
            dma((seqs - 1,)),
            dma((seqs - 1,)),
        ],
        compiler_params=pltpu.CompilerParams(collective_id=2, has_side_effects=True, vmem_limit_bytes=VMEM_LIMIT),
        name="project_return",
    )(attention, w_out, rows, gain)


def fast_body(tokens, new_tokens, w_qkv, w_out, q_gain, k_gain, post_gain, lengths):
    seqs, pos_dev, width = tokens.shape
    full = w_qkv.shape[1]
    shards = lax.axis_size("seq")
    group = shards // seqs
    piece = pos_dev // group
    me = lax.axis_index("seq")
    prompt, member = me // group, me % group
    count = shards * piece
    fresh = lax.dynamic_slice_in_dim(new_tokens, prompt, 1, 0)
    fresh = jnp.pad(fresh, ((0, PAD - 1), (0, 0)))
    rows, raw, value = call_gather(tokens.reshape(shards, piece, width), fresh, w_qkv, shards, piece)

    length = lax.dynamic_index_in_dim(lengths, prompt, 0, keepdims=False)
    index = jnp.arange(count, dtype=jnp.int32)

    def positions(who):
        return ((index // piece) ^ who) * pos_dev + (who % group) * piece + index % piece

    tail = jnp.arange(PAD, dtype=jnp.int32) == 0
    position = jnp.concatenate([positions(me), jnp.where(tail, length, 0)])
    cosine, sine = rope_tables(position)
    cos = jnp.concatenate([cosine, cosine], -1)
    sin = jnp.concatenate([-sine, sine], -1)
    key_pos = jnp.concatenate([positions(me), positions(me ^ 1)])
    key_pos = jnp.concatenate(
        [jnp.where(key_pos < length, key_pos, FAR + 1), jnp.where(tail, FAR, FAR + 1)]
    )
    query_pos = jnp.concatenate([positions(me), jnp.where(tail, FAR, 0)])
    attention = call_attend(
        full, raw, value, cos, sin, query_pos[:, None], key_pos[None, :], q_gain[None], k_gain[None]
    )
    out, new = call_project(full, shards, piece, group, attention, w_out, rows, post_gain[None])
    return out.reshape(seqs, pos_dev, width), new[:, 0]


def solution(mesh):
    in_specs = (
        P(None, "seq", "tp"),
        P(None, "tp"),
        P(None, None, "tp"),
        P("tp", None),
        P("tp"),
        P("tp"),
        P("tp"),
        P(),
    )
    out_specs = (P(None, "seq", "tp"), P(None, "tp"))
    chosen = fast_body if (mesh.shape["seq"], mesh.shape["tp"]) == (8, 4) else body
    return jax.shard_map(chosen, mesh=mesh, in_specs=in_specs, out_specs=out_specs, check_vma=False)
```

```python
from functools import partial

import jax
import jax.numpy as jnp
from jax import lax
from jax.experimental import pallas as pl
from jax.experimental.pallas import tpu as pltpu
from jax.sharding import PartitionSpec as P

HD = 128
PAD = 16
FAR = 1 << 30

rope_base = 500000.0
norm_eps = 1e-06
masked_fill = -1e30


def rope_tables(position):
    half = HD // 2
    freq = rope_base ** (-(jnp.arange(half, dtype=jnp.float32) * 2.0) / HD)
    angle = position.astype(jnp.float32)[:, None] * freq
    return jnp.cos(angle), jnp.sin(angle)


def rotate(values, cosine, sine):
    half = HD // 2
    lower = values[..., :half]
    upper = values[..., half:]
    return jnp.concatenate([lower * cosine - upper * sine, upper * cosine + lower * sine], -1)


def body(tokens, new_tokens, w_qkv, w_out, q_gain, k_gain, post_gain, lengths):
    seqs, pos_dev, width = tokens.shape
    heads = width // HD
    full = w_qkv.shape[1]
    shards = lax.axis_size("seq")
    group = shards // seqs
    piece = pos_dev // group
    me = lax.axis_index("seq")
    prompt, member = me // group, me % group
    count = shards * piece

    swapped = lax.all_to_all(tokens.reshape(shards, piece, width), "seq", 0, 0, tiled=True)
    fresh = lax.dynamic_slice_in_dim(new_tokens, prompt, 1, 0)
    rows = jnp.concatenate(
        [swapped.reshape(count, width), fresh, jnp.zeros((PAD - 1, width), tokens.dtype)], 0
    )
    everything = lax.all_gather(rows, "tp", axis=1, tiled=True)
    total = count + PAD
    proj = jnp.einsum("tn,cnf->ctf", everything, w_qkv, preferred_element_type=jnp.float32)
    squares = lax.psum(jnp.sum(proj[:2] * proj[:2], -1), "tp")
    factor = lax.rsqrt(squares / full + norm_eps)[..., None]

    length = lax.dynamic_index_in_dim(lengths, prompt, 0, keepdims=False)
    index = jnp.arange(count, dtype=jnp.int32)

    def positions(who):
        return (index // piece) * pos_dev + who * piece + index % piece

    tail = jnp.arange(PAD, dtype=jnp.int32) == 0
    position = jnp.concatenate([positions(member), jnp.where(tail, length, 0)])
    cosine, sine = rope_tables(position)
    cosine, sine = cosine[:, None], sine[:, None]

    def rotated(which, gain):
        normed = (proj[which] * factor[which] * gain).reshape(total, heads, HD)
        return rotate(normed, cosine, sine).astype(jnp.bfloat16)

    queries = rotated(0, q_gain)
    keys = rotated(1, k_gain)
    values = proj[2].astype(jnp.bfloat16).reshape(total, heads, HD)
    groups = [[b * group + g for g in range(group)] for b in range(seqs)]
    both = jnp.stack([keys[:count], values[:count]])
    gathered = lax.all_gather(both, "seq", axis=1, tiled=True, axis_index_groups=groups)
    all_keys = jnp.concatenate([gathered[0], keys[count:]], 0)
    all_values = jnp.concatenate([gathered[1], values[count:]], 0)
    key_pos = jnp.concatenate(
        [positions(g) for g in range(group)]
    )
    key_pos = jnp.concatenate([jnp.where(key_pos < length, key_pos, FAR + 1), jnp.where(tail, FAR, FAR + 1)])
    query_pos = jnp.concatenate([positions(member), jnp.where(tail, FAR, 0)])
    scores = jnp.einsum("phe,nhe->hpn", queries, all_keys, preferred_element_type=jnp.float32) * (
        HD ** (-0.5)
    )
    valid = (key_pos[None, :] <= query_pos[:, None])[None]
    scores = jnp.where(valid, scores, masked_fill)
    top = jnp.max(scores, -1, keepdims=True)
    weights = jnp.where(valid, jnp.exp(scores - top), 0.0)
    norm = jnp.sum(weights, -1)
    acc = jnp.einsum(
        "hpn,nhe->hpe", weights.astype(jnp.bfloat16), all_values, preferred_element_type=jnp.float32
    )
    attention = (acc / norm[..., None]).transpose(1, 0, 2).reshape(total, width).astype(jnp.bfloat16)

    part = jnp.dot(attention, w_out, preferred_element_type=jnp.float32).astype(jnp.bfloat16)
    own = lax.psum_scatter(part, "tp", scatter_dimension=1, tiled=True).astype(jnp.float32)
    mean = lax.psum(jnp.sum(own * own, -1), "tp") / full
    result = rows.astype(jnp.float32) + own * lax.rsqrt(mean[:, None] + norm_eps) * post_gain
    result = result.astype(jnp.bfloat16)
    out = lax.all_to_all(result[:count].reshape(shards, piece, width), "seq", 0, 0, tiled=True)
    new = lax.all_gather(result[count], "seq", axis=0)
    new = new.reshape(seqs, group, width)[:, 0]
    return out.reshape(seqs, pos_dev, width), new


MESH = pl.DeviceIdType.MESH
VMEM_LIMIT = 60 << 20
ROWS = 128


def remote(src, dst, send, recv, target):
    return pltpu.make_async_remote_copy(
        src_ref=src, dst_ref=dst, send_sem=send, recv_sem=recv, device_id=target, device_id_type=MESH
    )


def greet(targets):
    barrier = pltpu.get_barrier_semaphore()
    for target in targets:
        pl.semaphore_signal(barrier, inc=1, device_id=target, device_id_type=MESH)
    pl.semaphore_wait(barrier, len(targets))


def gather_project(shards, piece, tok, new, w, rows, raw, value, x, wv, acc, w_sem, loc_sem, a_send, a_recv, g_send, g_recv, n_send, n_recv):
    me, t = lax.axis_index("seq"), lax.axis_index("tp")
    width = tok.shape[2]
    count = shards * piece
    half = piece // 2
    near = [{"tp": t ^ j} for j in range(1, 4)]
    loads = []
    for j in range(4):
        load = pltpu.make_async_copy(w.at[:, pl.ds((t ^ j) * width, width), :], wv.at[j], w_sem.at[j])
        load.start()
        loads.append(load)
    own = pltpu.make_async_copy(tok.at[me], x.at[0, pl.ds(0, piece)], loc_sem.at[0])
    own.start()
    fresh = pltpu.make_async_copy(new, x.at[0, pl.ds(count, PAD)], loc_sem.at[1])
    fresh.start()
    greet([{"seq": me ^ k} for k in range(1, shards)] + near)

    swaps = []
    for k in range(1, shards):
        copy = remote(tok.at[me ^ k], x.at[0, pl.ds(k * piece, piece)], a_send.at[k], a_recv.at[k], {"seq": me ^ k})
        copy.start()
        swaps.append(copy)

    def first(j, k):
        at = x.at[0, pl.ds(k * piece, piece)]
        return remote(at, x.at[j, pl.ds(k * piece, piece)], g_send.at[j - 1, k], g_recv.at[j - 1, k], near[j - 1])

    def second(j, k):
        start = k * piece + (j - 1) * half
        return remote(
            x.at[j, pl.ds(start, half)], x.at[3, pl.ds(start, half)],
            g_send.at[1 + j, k], g_recv.at[1 + j, k], near[2 - j],
        )

    def tail(j):
        at = x.at[0, pl.ds(count, PAD)]
        return remote(at, x.at[j, pl.ds(count, PAD)], n_send.at[j - 1], n_recv.at[j - 1], near[j - 1])

    def multiply(j, start, size, clear):
        def tile(target, c, place, i):
            col = pl.ds(pl.multiple_of(i * (width // 2), width // 2), width // 2)
            part = jnp.dot(x[j, pl.ds(start, size), :], wv[j, c, :, col], preferred_element_type=jnp.float32)
            if clear:
                target[place, pl.ds(start, size), col] = part
            else:
                target[place, pl.ds(start, size), col] += part

        def scored(i, carry):
            tile(raw, i // 2, i // 2, i % 2)
            return carry

        def valued(i, carry):
            tile(acc, 2, 0, i)
            return carry

        lax.fori_loop(0, 4, scored, 0)
        lax.fori_loop(0, 2, valued, 0)

    def arrive(k):
        if k == 0:
            own.wait()
        else:
            swaps[k - 1].wait_recv()
        first(1, k).start()
        first(2, k).start()

    def forward(k):
        first(1, k).wait_recv()
        second(1, k).start()
        first(2, k).wait_recv()
        second(2, k).start()

    middle = shards // 2
    low, high = middle * piece, count - middle * piece + PAD
    for k in range(shards):
        arrive(k)
        if k == 0:
            fresh.wait()
            for j in range(1, 4):
                tail(j).start()
        if k >= 1 and k != middle:
            forward(k - 1)
        if k == middle - 1:
            loads[0].wait()
            multiply(0, 0, low, True)
            forward(k)
            loads[1].wait()
            multiply(1, 0, low, False)
            loads[2].wait()
            multiply(2, 0, low, False)
    multiply(0, low, high, True)
    forward(shards - 1)
    loads[3].wait()
    for k in range(middle):
        second(1, k).wait_recv()
        second(2, k).wait_recv()
    multiply(3, 0, low, False)
    for j in range(1, 4):
        tail(j).wait_recv()
    multiply(1, low, high, False)
    multiply(2, low, high, False)
    for k in range(middle, shards):
        second(1, k).wait_recv()
        second(2, k).wait_recv()
    multiply(3, low, high, False)
    value[...] = acc[0].astype(jnp.bfloat16)
    rows[...] = x[0]
    for copy in swaps:
        copy.wait_send()
    for k in range(shards):
        for j in (1, 2):
            first(j, k).wait_send()
            second(j, k).wait_send()
    for j in range(1, 4):
        tail(j).wait_send()


def flat_tile(column):
    size = column.shape[0]
    wide = jnp.broadcast_to(column, (size, ROWS))
    if size < ROWS:
        wide = jnp.concatenate([wide, jnp.zeros((ROWS - size, ROWS), jnp.float32)], 0)
    return wide.T[0:8]


def tall_tile(flat, size):
    return jnp.broadcast_to(flat[0:1], (ROWS, ROWS)).T[0:size]


def lanes(block):
    total = block[:, 0:HD]
    for h in range(1, block.shape[1] // HD):
        total = total + block[:, h * HD : (h + 1) * HD]
    return total


def attend(full, raw, value, cos, sin, qpos, kpos, qg, kg, out, sq, sq_in, q, ka, va, bias, s_send, s_recv, p_send, p_recv, loc_sem):
    me, t = lax.axis_index("seq"), lax.axis_index("tp")
    total, width = value.shape
    count = total - PAD
    heads = width // HD
    near = [{"tp": t ^ j} for j in range(1, 4)]
    mate = {"seq": me ^ 1}
    spans = [(i * ROWS, ROWS) for i in range(count // ROWS)] + [(count, PAD)]
    tiles = len(spans)
    greet(near + [mate])
    send_v = remote(value.at[pl.ds(0, count)], va.at[pl.ds(count, count)], p_send.at[0], p_recv.at[0], mate)
    send_v.start()
    for which in range(2):
        for i, (start, size) in enumerate(spans):
            block = raw[which, start : start + size, :]
            column = jnp.sum(lanes(block * block), -1, keepdims=True)
            sq[which * tiles + i] = flat_tile(column)
    squares = [remote(sq, sq_in.at[j], s_send.at[j], s_recv.at[j], near[j]) for j in range(3)]
    for copy in squares:
        copy.start()
    va[0:count, :] = value[0:count, :]
    va[2 * count :, :] = value[count:, :]
    for start, size in spans:
        bias[start : start + size, :] = jnp.where(kpos[...] <= qpos[start : start + size, :], 0.0, masked_fill)
    for copy in squares:
        copy.wait_recv()

    def finish(which, gain, start, size, i):
        slot = which * tiles + i
        flat = sq[slot] + sq_in[0, slot] + sq_in[1, slot] + sq_in[2, slot]
        factor = lax.rsqrt(tall_tile(flat, size) / full + norm_eps)
        c, s = cos[start : start + size, :], sin[start : start + size, :]
        parts = []
        for h in range(heads):
            at = slice(h * HD, (h + 1) * HD)
            normed = raw[which, start : start + size, at] * factor * gain[:, at]
            parts.append((normed * c + pltpu.roll(normed, HD // 2, 1) * s).astype(jnp.bfloat16))
        return jnp.concatenate(parts, -1)

    for i, (start, size) in enumerate(spans):
        place = start if start < count else 2 * count
        ka[place : place + size, :] = finish(1, kg, start, size, i)
    send_k = remote(ka.at[pl.ds(0, count)], ka.at[pl.ds(count, count)], p_send.at[1], p_recv.at[1], mate)
    send_k.start()
    for i, (start, size) in enumerate(spans):
        q[start : start + size, :] = finish(0, qg, start, size, i)
    send_v.wait_recv()
    send_k.wait_recv()

    def one_head(h, carry):
        at = pl.ds(pl.multiple_of(h * HD, HD), HD)
        for start, size in spans:
            scores = lax.dot_general(
                q[start : start + size, at], ka[:, at], (((1,), (1,)), ((), ())), preferred_element_type=jnp.float32
            )
            scores = scores + bias[start : start + size, :]
            top = jnp.max(scores, -1, keepdims=True)
            weights = jnp.exp((scores - top) * (HD ** (-0.5)))
            norm = jnp.sum(weights, -1, keepdims=True)
            mixed = jnp.dot(weights.astype(jnp.bfloat16), va[:, at], preferred_element_type=jnp.float32)
            out[start : start + size, at] = (mixed / norm).astype(jnp.bfloat16)
        return carry

    lax.fori_loop(0, heads, one_head, 0)
    for copy in squares:
        copy.wait_send()
    send_v.wait_send()
    send_k.wait_send()


def in_vmem():
    return pl.BlockSpec(memory_space=pltpu.VMEM)


def call_gather(tokens, new, w_qkv, shards, piece):
    width = tokens.shape[2]
    total = shards * piece + PAD
    dma = pltpu.SemaphoreType.DMA
    return pl.pallas_call(
        partial(gather_project, shards, piece),
        out_shape=(
            jax.ShapeDtypeStruct((total, width), jnp.bfloat16),
            jax.ShapeDtypeStruct((2, total, width), jnp.float32),
            jax.ShapeDtypeStruct((total, width), jnp.bfloat16),
        ),
        in_specs=[in_vmem(), in_vmem(), pl.BlockSpec(memory_space=pl.ANY)],
        out_specs=(in_vmem(), in_vmem(), in_vmem()),
        scratch_shapes=[
            pltpu.VMEM((4, total, width), jnp.bfloat16),
            pltpu.VMEM((4, 3, width, width), jnp.bfloat16),
            pltpu.VMEM((1, total, width), jnp.float32),
            dma((4,)),
            dma((2,)),
            dma((shards,)),
            dma((shards,)),
            dma((4, shards)),
            dma((4, shards)),
            dma((3,)),
            dma((3,)),
        ],
        compiler_params=pltpu.CompilerParams(collective_id=0, has_side_effects=True, vmem_limit_bytes=VMEM_LIMIT),
        name="gather_project",
    )(tokens, new, w_qkv)


def call_attend(full, raw, value, cos, sin, qpos, kpos, qg, kg):
    total, width = value.shape
    keys = 2 * (total - PAD) + PAD
    tiles = (total - PAD) // ROWS + 1
    dma = pltpu.SemaphoreType.DMA
    return pl.pallas_call(
        partial(attend, full),
        out_shape=jax.ShapeDtypeStruct((total, width), jnp.bfloat16),
        in_specs=[in_vmem()] * 8,
        out_specs=in_vmem(),
        scratch_shapes=[
            pltpu.VMEM((2 * tiles, 8, ROWS), jnp.float32),
            pltpu.VMEM((3, 2 * tiles, 8, ROWS), jnp.float32),
            pltpu.VMEM((total, width), jnp.bfloat16),
            pltpu.VMEM((keys, width), jnp.bfloat16),
            pltpu.VMEM((keys, width), jnp.bfloat16),
            pltpu.VMEM((total, keys), jnp.float32),
            dma((3,)),
            dma((3,)),
            dma((2,)),
            dma((2,)),
            dma((1,)),
        ],
        compiler_params=pltpu.CompilerParams(collective_id=1, has_side_effects=True, vmem_limit_bytes=VMEM_LIMIT),
        name="attend",
    )(raw, value, cos, sin, qpos, kpos, qg, kg)


def project_return(full, shards, piece, group, att, w, rows, gain, out, new, wv, d3, r3, s1, s2, r1, r2, p0, p1, p2, o, sq, sq_in, w_sem, l_sem, d_send, d_recv, m_send, m_recv, s_send, s_recv, z_send, z_recv, n_send, n_recv):
    me, t = lax.axis_index("seq"), lax.axis_index("tp")
    total, width = att.shape
    count = total - PAD
    prompt = me // group
    near = [{"tp": t ^ j} for j in range(1, 4)]
    loads = []
    for j in range(4):
        loads.append(pltpu.make_async_copy(w.at[:, pl.ds((t ^ j) * width, width)], wv.at[j], w_sem.at[j]))
    for j in (3, 2, 1, 0):
        loads[j].start()
    greet([{"seq": me ^ k} for k in range(1, shards)] + near)
    split = count // 2
    side = ROWS // 2
    spans = [(start, side, side) for start in range(split, count, ROWS)] + [(count, PAD, 0)]
    late = len(spans)
    spans += [(start, side, side) for start in range(split - ROWS, -1, -ROWS)]

    def product(j, start, size, target):
        def tile(i, carry):
            col = pl.ds(pl.multiple_of(i * (width // 2), width // 2), width // 2)
            part = jnp.dot(att[pl.ds(start, size), :], wv[j, :, col], preferred_element_type=jnp.float32)
            target[pl.ds(start, size), col] = part.astype(target.dtype)
            return carry

        lax.fori_loop(0, 2, tile, 0)

    def diagonal(i):
        start, a, b = spans[i]
        copies = [remote(d3.at[pl.ds(start, a)], r3.at[pl.ds(start, a)], d_send.at[0, i], d_recv.at[0, i], near[0])]
        if b:
            copies.append(
                remote(d3.at[pl.ds(start + a, b)], r3.at[pl.ds(start + a, b)], d_send.at[1, i], d_recv.at[1, i], near[1])
            )
        return copies

    def merged(i):
        start, a, b = spans[i]
        at = pl.ds(start, a + b)
        return [
            remote(s2.at[at], r2.at[at], m_send.at[1, i], m_recv.at[1, i], near[1]),
            remote(s1.at[at], r1.at[at], m_send.at[0, i], m_recv.at[0, i], near[0]),
        ]

    def merge(i):
        start, a, b = spans[i]
        first, last = slice(start, start + a), slice(start + a, start + a + b)
        copies, sums = diagonal(i), merged(i)
        copies[0].wait_recv()
        s2[first, :] = (p2[first, :] + r3[first, :].astype(jnp.float32)).astype(jnp.bfloat16)
        if b:
            s2[last, :] = p2[last, :].astype(jnp.bfloat16)
        sums[0].start()
        s1[first, :] = p1[first, :].astype(jnp.bfloat16)
        if b:
            copies[1].wait_recv()
            s1[last, :] = (p1[last, :] + r3[last, :].astype(jnp.float32)).astype(jnp.bfloat16)
        sums[1].start()

    high = count - split + PAD
    loads[3].wait()
    product(3, split, high, d3)
    for i in range(late):
        for copy in diagonal(i):
            copy.start()
    loads[2].wait()
    product(2, split, high, p2)
    loads[1].wait()
    product(1, split, high, p1)
    product(3, 0, split, d3)
    for i in range(late):
        merge(i)
    for i in range(late, len(spans)):
        for copy in diagonal(i):
            copy.start()
    product(2, 0, split, p2)
    product(1, 0, split, p1)
    loads[0].wait()
    product(0, split, high, p0)
    product(0, 0, split, p0)

    def squares(i):
        return [remote(sq.at[i], sq_in.at[j, i], s_send.at[j, i], s_recv.at[j, i], near[j]) for j in range(3)]

    def swap(k):
        return remote(o.at[pl.ds(k * piece, piece)], out.at[me], z_send.at[k], z_recv.at[k], {"seq": me ^ k})

    def fresh(m):
        return remote(o.at[pl.ds(count, PAD)], new.at[prompt], n_send.at[m - 1], n_recv.at[m - 1], {"seq": me ^ (m * group)})

    local = pltpu.make_async_copy(o.at[pl.ds(0, piece)], out.at[me], l_sem.at[0])
    local_new = pltpu.make_async_copy(o.at[pl.ds(count, PAD)], new.at[prompt], l_sem.at[1])

    def stage_one(i):
        start, a, b = spans[i]
        at = slice(start, start + a + b)
        for copy in merged(i):
            copy.wait_recv()
        own = p0[at, :] + r1[at, :].astype(jnp.float32) + r2[at, :].astype(jnp.float32)
        p0[at, :] = own
        sq[i] = flat_tile(jnp.sum(lanes(own * own), -1, keepdims=True))
        for copy in squares(i):
            copy.start()

    def stage_two(i):
        start, a, b = spans[i]
        at = slice(start, start + a + b)
        for copy in squares(i):
            copy.wait_recv()
        flat = sq[i] + sq_in[0, i] + sq_in[1, i] + sq_in[2, i]
        factor = lax.rsqrt(tall_tile(flat, a + b) / full + norm_eps)
        for h in range(width // HD):
            col = slice(h * HD, (h + 1) * HD)
            o[at, col] = (
                rows[at, col].astype(jnp.float32) + p0[at, col] * factor * gain[:, col]
            ).astype(jnp.bfloat16)
        if start == count:
            local_new.start()
            for m in range(1, shards // group):
                fresh(m).start()
        else:
            for k in range(start // piece, (start + a + b) // piece):
                if k == 0:
                    local.start()
                else:
                    swap(k).start()

    for i in range(late - 1):
        stage_one(i)
    merge(late)
    for i in range(late - 1):
        stage_two(i)
    for i in range(late + 1, len(spans)):
        merge(i)
    stage_one(late - 1)
    for i in range(late, len(spans)):
        stage_one(i)
        stage_two(i - 1)
    stage_two(len(spans) - 1)
    local.wait()
    local_new.wait()
    for k in range(1, shards):
        swap(k).wait()
    for m in range(1, shards // group):
        fresh(m).wait()
    for i in range(len(spans)):
        for copy in diagonal(i) + merged(i) + squares(i):
            copy.wait_send()


def call_project(full, shards, piece, group, attention, w_out, rows, gain):
    total, width = rows.shape
    seqs = shards // group
    tiles = (total - PAD) // ROWS + 1
    dma = pltpu.SemaphoreType.DMA
    half = pltpu.VMEM((total, width), jnp.bfloat16)
    wide = pltpu.VMEM((total, width), jnp.float32)
    return pl.pallas_call(
        partial(project_return, full, shards, piece, group),
        out_shape=(
            jax.ShapeDtypeStruct((shards, piece, width), jnp.bfloat16),
            jax.ShapeDtypeStruct((seqs, PAD, width), jnp.bfloat16),
        ),
        in_specs=[in_vmem(), pl.BlockSpec(memory_space=pl.ANY), in_vmem(), in_vmem()],
        out_specs=(in_vmem(), in_vmem()),
        scratch_shapes=[
            pltpu.VMEM((4, width, width), jnp.bfloat16),
            half, half, half, half, half, half,
            wide, wide, wide,
            half,
            pltpu.VMEM((tiles, 8, ROWS), jnp.float32),
            pltpu.VMEM((3, tiles, 8, ROWS), jnp.float32),
            dma((4,)),
            dma((2,)),
            dma((2, tiles)),
            dma((2, tiles)),
            dma((2, tiles)),
            dma((2, tiles)),
            dma((3, tiles)),
            dma((3, tiles)),
            dma((shards,)),
            dma((shards,)),
            dma((seqs - 1,)),
            dma((seqs - 1,)),
        ],
        compiler_params=pltpu.CompilerParams(collective_id=2, has_side_effects=True, vmem_limit_bytes=VMEM_LIMIT),
        name="project_return",
    )(attention, w_out, rows, gain)


def fast_body(tokens, new_tokens, w_qkv, w_out, q_gain, k_gain, post_gain, lengths):
    seqs, pos_dev, width = tokens.shape
    full = w_qkv.shape[1]
    shards = lax.axis_size("seq")
    group = shards // seqs
    piece = pos_dev // group
    me = lax.axis_index("seq")
    prompt, member = me // group, me % group
    count = shards * piece
    fresh = lax.dynamic_slice_in_dim(new_tokens, prompt, 1, 0)
    fresh = jnp.pad(fresh, ((0, PAD - 1), (0, 0)))
    rows, raw, value = call_gather(tokens.reshape(shards, piece, width), fresh, w_qkv, shards, piece)

    length = lax.dynamic_index_in_dim(lengths, prompt, 0, keepdims=False)
    index = jnp.arange(count, dtype=jnp.int32)

    def positions(who):
        return ((index // piece) ^ who) * pos_dev + (who % group) * piece + index % piece

    tail = jnp.arange(PAD, dtype=jnp.int32) == 0
    position = jnp.concatenate([positions(me), jnp.where(tail, length, 0)])
    cosine, sine = rope_tables(position)
    cos = jnp.concatenate([cosine, cosine], -1)
    sin = jnp.concatenate([-sine, sine], -1)
    key_pos = jnp.concatenate([positions(me), positions(me ^ 1)])
    key_pos = jnp.concatenate(
        [jnp.where(key_pos < length, key_pos, FAR + 1), jnp.where(tail, FAR, FAR + 1)]
    )
    query_pos = jnp.concatenate([positions(me), jnp.where(tail, FAR, 0)])
    attention = call_attend(
        full, raw, value, cos, sin, query_pos[:, None], key_pos[None, :], q_gain[None], k_gain[None]
    )
    out, new = call_project(full, shards, piece, group, attention, w_out, rows, post_gain[None])
    return out.reshape(seqs, pos_dev, width), new[:, 0]


def solution(mesh):
    in_specs = (
        P(None, "seq", "tp"),
        P(None, "tp"),
        P(None, None, "tp"),
        P("tp", None),
        P("tp"),
        P("tp"),
        P("tp"),
        P(),
    )
    out_specs = (P(None, "seq", "tp"), P(None, "tp"))
    chosen = fast_body if (mesh.shape["seq"], mesh.shape["tp"]) == (8, 4) else body
    return jax.shard_map(chosen, mesh=mesh, in_specs=in_specs, out_specs=out_specs, check_vma=False)
```

```python
from functools import partial

import jax
import jax.numpy as jnp
from jax import lax
from jax.experimental import pallas as pl
from jax.experimental.pallas import tpu as pltpu
from jax.sharding import PartitionSpec as P

HD = 128
PAD = 16
FAR = 1 << 30

rope_base = 500000.0
norm_eps = 1e-06
masked_fill = -1e30


def rope_tables(position):
    half = HD // 2
    freq = rope_base ** (-(jnp.arange(half, dtype=jnp.float32) * 2.0) / HD)
    angle = position.astype(jnp.float32)[:, None] * freq
    return jnp.cos(angle), jnp.sin(angle)


def rotate(values, cosine, sine):
    half = HD // 2
    lower = values[..., :half]
    upper = values[..., half:]
    return jnp.concatenate([lower * cosine - upper * sine, upper * cosine + lower * sine], -1)


def body(tokens, new_tokens, w_qkv, w_out, q_gain, k_gain, post_gain, lengths):
    seqs, pos_dev, width = tokens.shape
    heads = width // HD
    full = w_qkv.shape[1]
    shards = lax.axis_size("seq")
    group = shards // seqs
    piece = pos_dev // group
    me = lax.axis_index("seq")
    prompt, member = me // group, me % group
    count = shards * piece

    swapped = lax.all_to_all(tokens.reshape(shards, piece, width), "seq", 0, 0, tiled=True)
    fresh = lax.dynamic_slice_in_dim(new_tokens, prompt, 1, 0)
    rows = jnp.concatenate(
        [swapped.reshape(count, width), fresh, jnp.zeros((PAD - 1, width), tokens.dtype)], 0
    )
    everything = lax.all_gather(rows, "tp", axis=1, tiled=True)
    total = count + PAD
    proj = jnp.einsum("tn,cnf->ctf", everything, w_qkv, preferred_element_type=jnp.float32)
    squares = lax.psum(jnp.sum(proj[:2] * proj[:2], -1), "tp")
    factor = lax.rsqrt(squares / full + norm_eps)[..., None]

    length = lax.dynamic_index_in_dim(lengths, prompt, 0, keepdims=False)
    index = jnp.arange(count, dtype=jnp.int32)

    def positions(who):
        return (index // piece) * pos_dev + who * piece + index % piece

    tail = jnp.arange(PAD, dtype=jnp.int32) == 0
    position = jnp.concatenate([positions(member), jnp.where(tail, length, 0)])
    cosine, sine = rope_tables(position)
    cosine, sine = cosine[:, None], sine[:, None]

    def rotated(which, gain):
        normed = (proj[which] * factor[which] * gain).reshape(total, heads, HD)
        return rotate(normed, cosine, sine).astype(jnp.bfloat16)

    queries = rotated(0, q_gain)
    keys = rotated(1, k_gain)
    values = proj[2].astype(jnp.bfloat16).reshape(total, heads, HD)
    groups = [[b * group + g for g in range(group)] for b in range(seqs)]
    both = jnp.stack([keys[:count], values[:count]])
    gathered = lax.all_gather(both, "seq", axis=1, tiled=True, axis_index_groups=groups)
    all_keys = jnp.concatenate([gathered[0], keys[count:]], 0)
    all_values = jnp.concatenate([gathered[1], values[count:]], 0)
    key_pos = jnp.concatenate(
        [positions(g) for g in range(group)]
    )
    key_pos = jnp.concatenate([jnp.where(key_pos < length, key_pos, FAR + 1), jnp.where(tail, FAR, FAR + 1)])
    query_pos = jnp.concatenate([positions(member), jnp.where(tail, FAR, 0)])
    scores = jnp.einsum("phe,nhe->hpn", queries, all_keys, preferred_element_type=jnp.float32) * (
        HD ** (-0.5)
    )
    valid = (key_pos[None, :] <= query_pos[:, None])[None]
    scores = jnp.where(valid, scores, masked_fill)
    top = jnp.max(scores, -1, keepdims=True)
    weights = jnp.where(valid, jnp.exp(scores - top), 0.0)
    norm = jnp.sum(weights, -1)
    acc = jnp.einsum(
        "hpn,nhe->hpe", weights.astype(jnp.bfloat16), all_values, preferred_element_type=jnp.float32
    )
    attention = (acc / norm[..., None]).transpose(1, 0, 2).reshape(total, width).astype(jnp.bfloat16)

    part = jnp.dot(attention, w_out, preferred_element_type=jnp.float32).astype(jnp.bfloat16)
    own = lax.psum_scatter(part, "tp", scatter_dimension=1, tiled=True).astype(jnp.float32)
    mean = lax.psum(jnp.sum(own * own, -1), "tp") / full
    result = rows.astype(jnp.float32) + own * lax.rsqrt(mean[:, None] + norm_eps) * post_gain
    result = result.astype(jnp.bfloat16)
    out = lax.all_to_all(result[:count].reshape(shards, piece, width), "seq", 0, 0, tiled=True)
    new = lax.all_gather(result[count], "seq", axis=0)
    new = new.reshape(seqs, group, width)[:, 0]
    return out.reshape(seqs, pos_dev, width), new


MESH = pl.DeviceIdType.MESH
VMEM_LIMIT = 60 << 20
ROWS = 128


def remote(src, dst, send, recv, target):
    return pltpu.make_async_remote_copy(
        src_ref=src, dst_ref=dst, send_sem=send, recv_sem=recv, device_id=target, device_id_type=MESH
    )


def greet(targets):
    barrier = pltpu.get_barrier_semaphore()
    for target in targets:
        pl.semaphore_signal(barrier, inc=1, device_id=target, device_id_type=MESH)
    pl.semaphore_wait(barrier, len(targets))


def gather_project(shards, piece, tok, new, w, rows, raw, value, x, wv, acc, w_sem, loc_sem, a_send, a_recv, g_send, g_recv, n_send, n_recv):
    me, t = lax.axis_index("seq"), lax.axis_index("tp")
    width = tok.shape[2]
    count = shards * piece
    half = piece // 2
    near = [{"tp": t ^ j} for j in range(1, 4)]
    loads = []
    for j in range(4):
        load = pltpu.make_async_copy(w.at[:, pl.ds((t ^ j) * width, width), :], wv.at[j], w_sem.at[j])
        load.start()
        loads.append(load)
    own = pltpu.make_async_copy(tok.at[me], x.at[0, pl.ds(0, piece)], loc_sem.at[0])
    own.start()
    fresh = pltpu.make_async_copy(new, x.at[0, pl.ds(count, PAD)], loc_sem.at[1])
    fresh.start()
    greet([{"seq": me ^ k} for k in range(1, shards)] + near)

    swaps = []
    for k in range(1, shards):
        copy = remote(tok.at[me ^ k], x.at[0, pl.ds(k * piece, piece)], a_send.at[k], a_recv.at[k], {"seq": me ^ k})
        copy.start()
        swaps.append(copy)

    def first(j, k):
        at = x.at[0, pl.ds(k * piece, piece)]
        return remote(at, x.at[j, pl.ds(k * piece, piece)], g_send.at[j - 1, k], g_recv.at[j - 1, k], near[j - 1])

    def second(j, k):
        start = k * piece + (j - 1) * half
        return remote(
            x.at[j, pl.ds(start, half)], x.at[3, pl.ds(start, half)],
            g_send.at[1 + j, k], g_recv.at[1 + j, k], near[2 - j],
        )

    def tail(j):
        at = x.at[0, pl.ds(count, PAD)]
        return remote(at, x.at[j, pl.ds(count, PAD)], n_send.at[j - 1], n_recv.at[j - 1], near[j - 1])

    def multiply(j, start, size, clear):
        def tile(target, c, place, i):
            col = pl.ds(pl.multiple_of(i * (width // 2), width // 2), width // 2)
            part = jnp.dot(x[j, pl.ds(start, size), :], wv[j, c, :, col], preferred_element_type=jnp.float32)
            if clear:
                target[place, pl.ds(start, size), col] = part
            else:
                target[place, pl.ds(start, size), col] += part

        def scored(i, carry):
            tile(raw, i // 2, i // 2, i % 2)
            return carry

        def valued(i, carry):
            tile(acc, 2, 0, i)
            return carry

        lax.fori_loop(0, 4, scored, 0)
        lax.fori_loop(0, 2, valued, 0)

    def arrive(k):
        if k == 0:
            own.wait()
        else:
            swaps[k - 1].wait_recv()
        first(1, k).start()
        first(2, k).start()

    def forward(k):
        first(1, k).wait_recv()
        second(1, k).start()
        first(2, k).wait_recv()
        second(2, k).start()

    middle = shards // 2
    low, high = middle * piece, count - middle * piece + PAD
    for k in range(shards):
        arrive(k)
        if k == 0:
            fresh.wait()
            for j in range(1, 4):
                tail(j).start()
        if k >= 1 and k != middle:
            forward(k - 1)
        if k == middle - 1:
            loads[0].wait()
            multiply(0, 0, low, True)
            forward(k)
            loads[1].wait()
            multiply(1, 0, low, False)
            loads[2].wait()
            multiply(2, 0, low, False)
    multiply(0, low, high, True)
    forward(shards - 1)
    loads[3].wait()
    for k in range(middle):
        second(1, k).wait_recv()
        second(2, k).wait_recv()
    multiply(3, 0, low, False)
    for j in range(1, 4):
        tail(j).wait_recv()
    multiply(1, low, high, False)
    multiply(2, low, high, False)
    for k in range(middle, shards):
        second(1, k).wait_recv()
        second(2, k).wait_recv()
    multiply(3, low, high, False)
    value[...] = acc[0].astype(jnp.bfloat16)
    rows[...] = x[0]
    for copy in swaps:
        copy.wait_send()
    for k in range(shards):
        for j in (1, 2):
            first(j, k).wait_send()
            second(j, k).wait_send()
    for j in range(1, 4):
        tail(j).wait_send()


def flat_tile(column):
    size = column.shape[0]
    wide = jnp.broadcast_to(column, (size, ROWS))
    if size < ROWS:
        wide = jnp.concatenate([wide, jnp.zeros((ROWS - size, ROWS), jnp.float32)], 0)
    return wide.T[0:8]


def tall_tile(flat, size):
    return jnp.broadcast_to(flat[0:1], (ROWS, ROWS)).T[0:size]


def lanes(block):
    total = block[:, 0:HD]
    for h in range(1, block.shape[1] // HD):
        total = total + block[:, h * HD : (h + 1) * HD]
    return total


def attend(full, raw, value, cos, sin, qpos, kpos, qg, kg, out, sq, sq_in, q, ka, va, bias, s_send, s_recv, p_send, p_recv, loc_sem):
    me, t = lax.axis_index("seq"), lax.axis_index("tp")
    total, width = value.shape
    count = total - PAD
    heads = width // HD
    near = [{"tp": t ^ j} for j in range(1, 4)]
    mate = {"seq": me ^ 1}
    spans = [(i * ROWS, ROWS) for i in range(count // ROWS)] + [(count, PAD)]
    tiles = len(spans)
    greet(near + [mate])
    send_v = remote(value.at[pl.ds(0, count)], va.at[pl.ds(count, count)], p_send.at[0], p_recv.at[0], mate)
    send_v.start()
    for which in range(2):
        for i, (start, size) in enumerate(spans):
            block = raw[which, start : start + size, :]
            column = jnp.sum(lanes(block * block), -1, keepdims=True)
            sq[which * tiles + i] = flat_tile(column)
    squares = [remote(sq, sq_in.at[j], s_send.at[j], s_recv.at[j], near[j]) for j in range(3)]
    for copy in squares:
        copy.start()
    va[0:count, :] = value[0:count, :]
    va[2 * count :, :] = value[count:, :]
    for start, size in spans:
        bias[start : start + size, :] = jnp.where(kpos[...] <= qpos[start : start + size, :], 0.0, masked_fill)
    for copy in squares:
        copy.wait_recv()

    def finish(which, gain, start, size, i):
        slot = which * tiles + i
        flat = sq[slot] + sq_in[0, slot] + sq_in[1, slot] + sq_in[2, slot]
        factor = lax.rsqrt(tall_tile(flat, size) / full + norm_eps)
        c, s = cos[start : start + size, :], sin[start : start + size, :]
        parts = []
        for h in range(heads):
            at = slice(h * HD, (h + 1) * HD)
            normed = raw[which, start : start + size, at] * factor * gain[:, at]
            parts.append((normed * c + pltpu.roll(normed, HD // 2, 1) * s).astype(jnp.bfloat16))
        return jnp.concatenate(parts, -1)

    for i, (start, size) in enumerate(spans):
        place = start if start < count else 2 * count
        ka[place : place + size, :] = finish(1, kg, start, size, i)
    send_k = remote(ka.at[pl.ds(0, count)], ka.at[pl.ds(count, count)], p_send.at[1], p_recv.at[1], mate)
    send_k.start()
    for i, (start, size) in enumerate(spans):
        q[start : start + size, :] = finish(0, qg, start, size, i)
    send_v.wait_recv()
    send_k.wait_recv()

    def one_head(h, carry):
        at = pl.ds(pl.multiple_of(h * HD, HD), HD)
        for start, size in spans:
            scores = lax.dot_general(
                q[start : start + size, at], ka[:, at], (((1,), (1,)), ((), ())), preferred_element_type=jnp.float32
            )
            scores = scores + bias[start : start + size, :]
            top = jnp.max(scores, -1, keepdims=True)
            weights = jnp.exp2((scores - top) * (HD ** (-0.5) * 1.4426950408889634))
            norm = jnp.sum(weights, -1, keepdims=True)
            mixed = jnp.dot(weights.astype(jnp.bfloat16), va[:, at], preferred_element_type=jnp.float32)
            out[start : start + size, at] = (mixed / norm).astype(jnp.bfloat16)
        return carry

    lax.fori_loop(0, heads, one_head, 0, unroll=2)
    for copy in squares:
        copy.wait_send()
    send_v.wait_send()
    send_k.wait_send()


def in_vmem():
    return pl.BlockSpec(memory_space=pltpu.VMEM)


def call_gather(tokens, new, w_qkv, shards, piece):
    width = tokens.shape[2]
    total = shards * piece + PAD
    dma = pltpu.SemaphoreType.DMA
    return pl.pallas_call(
        partial(gather_project, shards, piece),
        out_shape=(
            jax.ShapeDtypeStruct((total, width), jnp.bfloat16),
            jax.ShapeDtypeStruct((2, total, width), jnp.float32),
            jax.ShapeDtypeStruct((total, width), jnp.bfloat16),
        ),
        in_specs=[in_vmem(), in_vmem(), pl.BlockSpec(memory_space=pl.ANY)],
        out_specs=(in_vmem(), in_vmem(), in_vmem()),
        scratch_shapes=[
            pltpu.VMEM((4, total, width), jnp.bfloat16),
            pltpu.VMEM((4, 3, width, width), jnp.bfloat16),
            pltpu.VMEM((1, total, width), jnp.float32),
            dma((4,)),
            dma((2,)),
            dma((shards,)),
            dma((shards,)),
            dma((4, shards)),
            dma((4, shards)),
            dma((3,)),
            dma((3,)),
        ],
        compiler_params=pltpu.CompilerParams(collective_id=0, has_side_effects=True, vmem_limit_bytes=VMEM_LIMIT),
        name="gather_project",
    )(tokens, new, w_qkv)


def call_attend(full, raw, value, cos, sin, qpos, kpos, qg, kg):
    total, width = value.shape
    keys = 2 * (total - PAD) + PAD
    tiles = (total - PAD) // ROWS + 1
    dma = pltpu.SemaphoreType.DMA
    return pl.pallas_call(
        partial(attend, full),
        out_shape=jax.ShapeDtypeStruct((total, width), jnp.bfloat16),
        in_specs=[in_vmem()] * 8,
        out_specs=in_vmem(),
        scratch_shapes=[
            pltpu.VMEM((2 * tiles, 8, ROWS), jnp.float32),
            pltpu.VMEM((3, 2 * tiles, 8, ROWS), jnp.float32),
            pltpu.VMEM((total, width), jnp.bfloat16),
            pltpu.VMEM((keys, width), jnp.bfloat16),
            pltpu.VMEM((keys, width), jnp.bfloat16),
            pltpu.VMEM((total, keys), jnp.float32),
            dma((3,)),
            dma((3,)),
            dma((2,)),
            dma((2,)),
            dma((1,)),
        ],
        compiler_params=pltpu.CompilerParams(collective_id=1, has_side_effects=True, vmem_limit_bytes=VMEM_LIMIT),
        name="attend",
    )(raw, value, cos, sin, qpos, kpos, qg, kg)


def project_return(full, shards, piece, group, att, w, rows, gain, out, new, wv, d3, r3, s1, s2, r1, r2, p0, p1, p2, o, sq, sq_in, w_sem, l_sem, d_send, d_recv, m_send, m_recv, s_send, s_recv, z_send, z_recv, n_send, n_recv):
    me, t = lax.axis_index("seq"), lax.axis_index("tp")
    total, width = att.shape
    count = total - PAD
    prompt = me // group
    near = [{"tp": t ^ j} for j in range(1, 4)]
    loads = []
    for j in range(4):
        loads.append(pltpu.make_async_copy(w.at[:, pl.ds((t ^ j) * width, width)], wv.at[j], w_sem.at[j]))
    for j in (3, 2, 1, 0):
        loads[j].start()
    greet([{"seq": me ^ k} for k in range(1, shards)] + near)
    split = count // 2
    side = ROWS // 2
    spans = [(start, side, side) for start in range(split, count, ROWS)] + [(count, PAD, 0)]
    late = len(spans)
    spans += [(start, side, side) for start in range(split - ROWS, -1, -ROWS)]

    def product(j, start, size, target):
        def tile(i, carry):
            col = pl.ds(pl.multiple_of(i * (width // 2), width // 2), width // 2)
            part = jnp.dot(att[pl.ds(start, size), :], wv[j, :, col], preferred_element_type=jnp.float32)
            target[pl.ds(start, size), col] = part.astype(target.dtype)
            return carry

        lax.fori_loop(0, 2, tile, 0)

    def diagonal(i):
        start, a, b = spans[i]
        copies = [remote(d3.at[pl.ds(start, a)], r3.at[pl.ds(start, a)], d_send.at[0, i], d_recv.at[0, i], near[0])]
        if b:
            copies.append(
                remote(d3.at[pl.ds(start + a, b)], r3.at[pl.ds(start + a, b)], d_send.at[1, i], d_recv.at[1, i], near[1])
            )
        return copies

    def merged(i):
        start, a, b = spans[i]
        at = pl.ds(start, a + b)
        return [
            remote(s2.at[at], r2.at[at], m_send.at[1, i], m_recv.at[1, i], near[1]),
            remote(s1.at[at], r1.at[at], m_send.at[0, i], m_recv.at[0, i], near[0]),
        ]

    def merge(i):
        start, a, b = spans[i]
        first, last = slice(start, start + a), slice(start + a, start + a + b)
        copies, sums = diagonal(i), merged(i)
        copies[0].wait_recv()
        s2[first, :] = (p2[first, :] + r3[first, :].astype(jnp.float32)).astype(jnp.bfloat16)
        if b:
            s2[last, :] = p2[last, :].astype(jnp.bfloat16)
        sums[0].start()
        s1[first, :] = p1[first, :].astype(jnp.bfloat16)
        if b:
            copies[1].wait_recv()
            s1[last, :] = (p1[last, :] + r3[last, :].astype(jnp.float32)).astype(jnp.bfloat16)
        sums[1].start()

    high = count - split + PAD
    loads[3].wait()
    product(3, split, high, d3)
    for i in range(late):
        for copy in diagonal(i):
            copy.start()
    loads[2].wait()
    product(2, split, high, p2)
    loads[1].wait()
    product(1, split, high, p1)
    product(3, 0, split, d3)
    for i in range(late):
        merge(i)
    for i in range(late, len(spans)):
        for copy in diagonal(i):
            copy.start()
    product(2, 0, split, p2)
    product(1, 0, split, p1)
    loads[0].wait()
    product(0, split, high, p0)
    product(0, 0, split, p0)

    def squares(i):
        return [remote(sq.at[i], sq_in.at[j, i], s_send.at[j, i], s_recv.at[j, i], near[j]) for j in range(3)]

    def swap(k):
        return remote(o.at[pl.ds(k * piece, piece)], out.at[me], z_send.at[k], z_recv.at[k], {"seq": me ^ k})

    def fresh(m):
        return remote(o.at[pl.ds(count, PAD)], new.at[prompt], n_send.at[m - 1], n_recv.at[m - 1], {"seq": me ^ (m * group)})

    local = pltpu.make_async_copy(o.at[pl.ds(0, piece)], out.at[me], l_sem.at[0])
    local_new = pltpu.make_async_copy(o.at[pl.ds(count, PAD)], new.at[prompt], l_sem.at[1])

    def stage_one(i):
        start, a, b = spans[i]
        at = slice(start, start + a + b)
        for copy in merged(i):
            copy.wait_recv()
        own = p0[at, :] + r1[at, :].astype(jnp.float32) + r2[at, :].astype(jnp.float32)
        p0[at, :] = own
        sq[i] = flat_tile(jnp.sum(lanes(own * own), -1, keepdims=True))
        for copy in squares(i):
            copy.start()

    def stage_two(i):
        start, a, b = spans[i]
        at = slice(start, start + a + b)
        for copy in squares(i):
            copy.wait_recv()
        flat = sq[i] + sq_in[0, i] + sq_in[1, i] + sq_in[2, i]
        factor = lax.rsqrt(tall_tile(flat, a + b) / full + norm_eps)
        for h in range(width // HD):
            col = slice(h * HD, (h + 1) * HD)
            o[at, col] = (
                rows[at, col].astype(jnp.float32) + p0[at, col] * factor * gain[:, col]
            ).astype(jnp.bfloat16)
        if start == count:
            local_new.start()
            for m in range(1, shards // group):
                fresh(m).start()
        else:
            for k in range(start // piece, (start + a + b) // piece):
                if k == 0:
                    local.start()
                else:
                    swap(k).start()

    for i in range(late - 1):
        stage_one(i)
    merge(late)
    for i in range(late - 1):
        stage_two(i)
    for i in range(late + 1, len(spans)):
        merge(i)
    stage_one(late - 1)
    for i in range(late, len(spans)):
        stage_one(i)
        stage_two(i - 1)
    stage_two(len(spans) - 1)
    local.wait()
    local_new.wait()
    for k in range(1, shards):
        swap(k).wait()
    for m in range(1, shards // group):
        fresh(m).wait()
    for i in range(len(spans)):
        for copy in diagonal(i) + merged(i) + squares(i):
            copy.wait_send()


def call_project(full, shards, piece, group, attention, w_out, rows, gain):
    total, width = rows.shape
    seqs = shards // group
    tiles = (total - PAD) // ROWS + 1
    dma = pltpu.SemaphoreType.DMA
    half = pltpu.VMEM((total, width), jnp.bfloat16)
    wide = pltpu.VMEM((total, width), jnp.float32)
    return pl.pallas_call(
        partial(project_return, full, shards, piece, group),
        out_shape=(
            jax.ShapeDtypeStruct((shards, piece, width), jnp.bfloat16),
            jax.ShapeDtypeStruct((seqs, PAD, width), jnp.bfloat16),
        ),
        in_specs=[in_vmem(), pl.BlockSpec(memory_space=pl.ANY), in_vmem(), in_vmem()],
        out_specs=(in_vmem(), in_vmem()),
        scratch_shapes=[
            pltpu.VMEM((4, width, width), jnp.bfloat16),
            half, half, half, half, half, half,
            wide, wide, wide,
            half,
            pltpu.VMEM((tiles, 8, ROWS), jnp.float32),
            pltpu.VMEM((3, tiles, 8, ROWS), jnp.float32),
            dma((4,)),
            dma((2,)),
            dma((2, tiles)),
            dma((2, tiles)),
            dma((2, tiles)),
            dma((2, tiles)),
            dma((3, tiles)),
            dma((3, tiles)),
            dma((shards,)),
            dma((shards,)),
            dma((seqs - 1,)),
            dma((seqs - 1,)),
        ],
        compiler_params=pltpu.CompilerParams(collective_id=2, has_side_effects=True, vmem_limit_bytes=VMEM_LIMIT),
        name="project_return",
    )(attention, w_out, rows, gain)


def fast_body(tokens, new_tokens, w_qkv, w_out, q_gain, k_gain, post_gain, lengths):
    seqs, pos_dev, width = tokens.shape
    full = w_qkv.shape[1]
    shards = lax.axis_size("seq")
    group = shards // seqs
    piece = pos_dev // group
    me = lax.axis_index("seq")
    prompt, member = me // group, me % group
    count = shards * piece
    fresh = lax.dynamic_slice_in_dim(new_tokens, prompt, 1, 0)
    fresh = jnp.pad(fresh, ((0, PAD - 1), (0, 0)))
    rows, raw, value = call_gather(tokens.reshape(shards, piece, width), fresh, w_qkv, shards, piece)

    length = lax.dynamic_index_in_dim(lengths, prompt, 0, keepdims=False)
    index = jnp.arange(count, dtype=jnp.int32)

    def positions(who):
        return ((index // piece) ^ who) * pos_dev + (who % group) * piece + index % piece

    tail = jnp.arange(PAD, dtype=jnp.int32) == 0
    position = jnp.concatenate([positions(me), jnp.where(tail, length, 0)])
    cosine, sine = rope_tables(position)
    cos = jnp.concatenate([cosine, cosine], -1)
    sin = jnp.concatenate([-sine, sine], -1)
    key_pos = jnp.concatenate([positions(me), positions(me ^ 1)])
    key_pos = jnp.concatenate(
        [jnp.where(key_pos < length, key_pos, FAR + 1), jnp.where(tail, FAR, FAR + 1)]
    )
    query_pos = jnp.concatenate([positions(me), jnp.where(tail, FAR, 0)])
    attention = call_attend(
        full, raw, value, cos, sin, query_pos[:, None], key_pos[None, :], q_gain[None], k_gain[None]
    )
    out, new = call_project(full, shards, piece, group, attention, w_out, rows, post_gain[None])
    return out.reshape(seqs, pos_dev, width), new[:, 0]


def solution(mesh):
    in_specs = (
        P(None, "seq", "tp"),
        P(None, "tp"),
        P(None, None, "tp"),
        P("tp", None),
        P("tp"),
        P("tp"),
        P("tp"),
        P(),
    )
    out_specs = (P(None, "seq", "tp"), P(None, "tp"))
    chosen = fast_body if (mesh.shape["seq"], mesh.shape["tp"]) == (8, 4) else body
    return jax.shard_map(chosen, mesh=mesh, in_specs=in_specs, out_specs=out_specs, check_vma=False)
```
